512 devices in a mesh: rep: 16 (over x_hi, z), fsdp: 32 (over x_lo, y, core).
Axes of the slice: x: 4 (x_hi: 2, x_lo: 2; x = x_hi * 2 + x_lo), y: 8, z: 8, core: 2. Of those that a mesh axis runs over, the one named last changes fastest.
Arguments:
- inputs: bfloat16 [16, 4096, 4608], P('rep', 'fsdp'), may hold values from -60 to 60, as said below
- targets: bfloat16 [16, 4096, 1024], P('rep', 'fsdp'), may hold values from -6 to 6
- local_weights: float32 [16, 4608, 1024], P('rep', 'fsdp'), may hold values from -6 to 6
- global_weights: float32 [4608, 128], P('fsdp'), may hold values from -6 to 6
- momentum: float32 [4608, 128], P('fsdp'), may hold values from -3 to 3
- fragment: int32 [1], replicated, may hold values from 0 to 4095
Outputs:
- new_local: float32 [16, 4608, 1024], P('rep', 'fsdp')
- input_grad: bfloat16 [16, 4096, 4608], P('rep', 'fsdp')
- new_momentum: float32 [4608, 128], P('fsdp')
- new_global: float32 [4608, 128], P('fsdp')
The draws below stay inside these ranges and needn't reach their ends.
Inputs may be any that keep to these rules, and one draw needn't show every extreme that they name: `inputs`: finite values.
All inputs are finite; a program needn't handle non-finite values.
Results may differ from the reference program's by a relative error of at most 0.0058.
Values may be sent and summed in bfloat16 or wider, within the bound.
A program may use at most 64 MiB of HBM per device.

```python
import math
import jax
import jax.numpy as jnp
from jax import lax

D = 4608
FRAGS = 8
TOKENS = 4096
H = 1024
FH = 128
N_REP = 16


def draw_inputs(key, part):
    key = jax.random.fold_in(key, 11)
    key_base, key_rows, key_cols = jax.random.split(key, 3)
    shape = (N_REP, TOKENS, D)
    row_scale = jnp.exp(jax.random.uniform(key_rows, (N_REP, TOKENS, 1), jnp.float32, math.log(0.3), math.log(3.0)))
    base = jnp.clip(jax.random.normal(key_base, shape, jnp.float32), -6.0, 6.0)
    col_scale = jnp.exp(jax.random.uniform(key_cols, (1, 1, D), jnp.float32, math.log(0.3), math.log(3.0)))
    return (base * row_scale * col_scale).astype(jnp.bfloat16)


def block_scale(key, extent, cuts, smallest, high):
    gain, own = 1.0, jax.random.fold_in(key, 6)
    for position, shards_of in cuts:
        draws = jnp.exp(jax.random.uniform(jax.random.fold_in(own, position), (shards_of,), jnp.float32, smallest / len(cuts), high / len(cuts)))
        gain = gain * jnp.repeat(draws, extent[position] // shards_of).reshape([-1 if axis == position else 1 for axis in range(len(extent))])
    return gain


def scatter_about(stream_key, dims, scale, limit, shards=(), kind=jnp.bfloat16):
    factor_of = block_scale(stream_key, dims, shards, -0.22, 0.18) if shards else 1.0
    array = jax.random.normal(stream_key, dims, jnp.float32) * scale * factor_of
    return jnp.minimum(jnp.maximum(array, -limit), limit).astype(kind)


def setup_inputs(seed: int = 0) -> dict:
    keys = jax.random.split(jax.random.key(seed), 7)
    inputs = draw_inputs(jax.random.fold_in(keys[6], 71), 0)
    targets = scatter_about(keys[1], (N_REP, TOKENS, H), 1.0, 6.0, ((0, 16), (1, 32)))
    local_weights = scatter_about(keys[2], (N_REP, D, H), 1.0, 6.0, ((0, 16), (1, 32)), jnp.float32)
    global_weights = scatter_about(keys[3], (D, FH), 1.0, 6.0, ((0, 32),), jnp.float32)
    momentum = scatter_about(keys[4], (D, FH), 0.5, 3.0, ((0, 32),), jnp.float32)
    fragment = jax.random.randint(keys[5], (1,), 0, 4096).astype(jnp.int32)
    return {"inputs": inputs, "targets": targets, "local_weights": local_weights, "global_weights": global_weights, "momentum": momentum, "fragment": fragment}


inner_rate = 0.2
outer_rate = 0.7
momentum_decay = 0.9
blend_keep = 0.5

def reference(inputs, targets, local_weights, global_weights, momentum, fragment):
    root = math.sqrt(TOKENS)
    out_root = math.sqrt(H)

    def replica_step(packed):
        rows_in, grads_in, weights = packed
        values = rows_in.astype(jnp.float32)
        scale = lax.rsqrt(lax.optimization_barrier(jnp.mean(values * values, axis=-1, keepdims=True)) + 1e-06)
        unrounded = values * scale
        normed = unrounded.astype(jnp.bfloat16)
        grad = jnp.dot(normed.T, grads_in, preferred_element_type=jnp.float32)
        weights_half = weights.astype(jnp.bfloat16)
        d_raw = jnp.dot(grads_in, weights_half.T, preferred_element_type=jnp.float32) / out_root
        d_normed = d_raw.astype(jnp.bfloat16).astype(jnp.float32)
        inner_prod = lax.optimization_barrier(jnp.mean(d_normed * unrounded, axis=-1, keepdims=True))
        input_grad = (scale * (d_normed - unrounded * inner_prod)).astype(jnp.bfloat16)
        return (weights - inner_rate * grad / root, input_grad)
    inner, input_grad = lax.map(replica_step, (inputs, targets, local_weights))
    start = fragment[0].astype(jnp.int32) % FRAGS * FH
    frag_local = lax.dynamic_slice_in_dim(local_weights, start, FH, 2)
    mean_delta = lax.optimization_barrier(jnp.sum(global_weights[None] - frag_local, axis=0)) / N_REP
    new_momentum = momentum_decay * momentum + mean_delta
    new_global = global_weights - outer_rate * (mean_delta + momentum_decay * new_momentum)
    frag_inner = lax.dynamic_slice_in_dim(inner, start, FH, 2)
    blended = blend_keep * frag_inner + (1.0 - blend_keep) * new_global[None]
    new_local = lax.dynamic_update_slice_in_dim(inner, blended, start, 2)
    return (new_local, input_grad, new_momentum, new_global)
```

```python
import functools
import math

import jax
import jax.numpy as jnp
from jax import lax
from jax.experimental import pallas as pl
from jax.experimental.pallas import tpu as pltpu
from jax.sharding import PartitionSpec as P

MESH = pl.DeviceIdType.MESH
bf16 = jnp.bfloat16
f32 = jnp.float32

inner_rate = 0.2
outer_rate = 0.7
momentum_decay = 0.9
blend_keep = 0.5


def kernel(
    n_rep, n_y, tokens_all,
    frag_ref, x_ref, t_ref, lw_ref, gw_ref, mom_ref,
    nl_ref, ig_ref, nm_ref, ng_ref,
    wown, wg, tg, nown, nrm, nT, G, dout, din, rsA, rsB, rsout, gtot, gsend, scale_ref, racc, rin,
    w_snd, w_rcv, wp_snd, tg_snd, tg_rcv, n_snd, n_rcv, d_snd, d_rcv,
    rs_snd, rsA_rcv, rsB_rcv, tot_snd, tot_rcv, r_snd, r_rcv,
):
    rep = lax.axis_index("rep")
    me = lax.axis_index("fsdp")
    half = n_y // 2
    c = lax.rem(me, 2)
    y = lax.rem(me // 2, n_y)
    xl = me // (2 * n_y)
    a = xl * 2 + c
    rows, hidden = lw_ref.shape
    tok, width = x_ref.shape
    quarter = width // 4
    origin = y // half == c

    def dev(x_, y_, c_):
        return x_ * (2 * n_y) + y_ * 2 + c_

    up = dev(xl, lax.rem(y + 1, n_y), c)
    dn = dev(xl, lax.rem(y + n_y - 1, n_y), c)
    mate = dev(xl, y, 1 - c)
    across = dev(1 - xl, y, c)
    diag = dev(1 - xl, y, 1 - c)
    a_mate, a_across, a_diag = xl * 2 + 1 - c, (1 - xl) * 2 + c, (1 - xl) * 2 + 1 - c

    masks = []
    m = n_rep // 2
    while m:
        masks.append(m)
        m //= 2
    rep_peers = [rep + m * (1 - 2 * lax.rem(rep // m, 2)) for m in masks]

    def copy(src, dst, ss, rs, to, r=None):
        return pltpu.make_async_remote_copy(
            src_ref=src, dst_ref=dst, send_sem=ss, recv_sem=rs,
            device_id=(rep if r is None else r, to), device_id_type=MESH,
        )

    def blk(ref, j):
        return ref.at[pl.ds(pl.multiple_of(j * rows, 16), rows), :]

    def ds_blk(j):
        return pl.ds(pl.multiple_of(j * rows, 16), rows)

    def tok_ds(k, n=1):
        return pl.ds(pl.multiple_of(k * tok, 16), n * tok)

    barrier = pltpu.get_barrier_semaphore()
    for peer in (up, dn, mate, across, diag):
        pl.semaphore_signal(barrier, inc=1, device_id=(rep, peer), device_id_type=MESH)
    for peer in rep_peers:
        pl.semaphore_signal(barrier, inc=1, device_id=(peer, me), device_id_type=MESH)
    pl.semaphore_wait(barrier, 5 + len(rep_peers))

    def slot(o, f):
        return 2 * (o - half * c) + (c if f == 0 else 1 - c)

    wown[...] = lw_ref[...].astype(bf16)
    j0 = 2 * (y - half * c) + c
    j1 = 2 * (y - half * c) + 1 - c
    jm = 2 * (y - half * (1 - c)) + c

    @pl.when(origin)
    def _():
        copy(wown, blk(wg, j0), w_snd.at[0, j0], w_rcv.at[j0], up).start()
        copy(wown, blk(wg, j0), w_snd.at[1, j0], w_rcv.at[j0], dn).start()

    @pl.when(jnp.logical_not(origin))
    def _():
        copy(wown, blk(wg, jm), wp_snd, w_rcv.at[jm], mate).start()

    tg[tok_ds(a), :] = t_ref[...]

    def tblk(k):
        return tg.at[tok_ds(k), :]

    copy(tblk(a), tblk(a), tg_snd.at[0], tg_rcv.at[a], across).start()
    copy(tblk(a), tblk(a), tg_snd.at[1], tg_rcv.at[a], mate).start()

    @pl.when(origin)
    def _():
        wg[ds_blk(j0), :] = wown[...]

    step = 16

    def norm_rows(i, _):
        r = pl.ds(pl.multiple_of(i * step, step), step)
        v = x_ref[r, :].astype(f32)
        sc = lax.rsqrt(jnp.sum(v * v, axis=-1, keepdims=True) * (1.0 / width) + 1e-06)
        scale_ref[r, :] = sc
        nv = (v * sc).astype(bf16)
        for k in range(4):
            nown[k, r, :] = nv[:, k * quarter : (k + 1) * quarter]
        return 0

    lax.fori_loop(0, tok // step, norm_rows, 0)

    def nblk(k):
        return nrm.at[tok_ds(k), :]

    n_copies = [
        copy(nown.at[k], nblk(a), n_snd.at[k], n_rcv.at[a], to)
        for k, to in ((a_across, across), (a_diag, diag), (a_mate, mate))
    ]
    for cp in n_copies:
        cp.start()
    nrm[tok_ds(a), :] = nown[a]

    picked = jnp.full((rows, 128), lax.rem(frag_ref[0], hidden // 128), jnp.int32)
    frag_local = lw_ref[:, :128]
    for k in range(1, hidden // 128):
        frag_local = jnp.where(picked == k, lw_ref[:, k * 128 : (k + 1) * 128], frag_local)
    racc[0] = gw_ref[...] - frag_local

    def r_copy(i):
        return copy(racc.at[i], rin.at[i], r_snd.at[i], r_rcv.at[i], me, rep_peers[i])

    r_copy(0).start()

    def rep_step(i):
        if i < len(masks):
            r_copy(i).wait_recv()
            racc[i + 1] = racc[i] + rin[i]
            if i + 1 < len(masks):
                r_copy(i + 1).start()

    @pl.when(origin)
    def _():
        first = copy(blk(wg, j1), blk(wg, j1), w_snd.at[0, j1], w_rcv.at[j1], up)
        first.wait_recv()
        first.start()
        copy(blk(wg, j1), blk(wg, j1), w_snd.at[1, j1], w_rcv.at[j1], dn).start()

    def ways(f):
        return ((1, half - f, up, 0), (-1, half - 1 + f, dn, 1))

    def gather_step(s):
        for f in (0, 1):
            for sign, hops, to, d in ways(f):
                if s > hops:
                    continue
                o = lax.rem(y - sign * s + n_y, n_y)

                @pl.when(o // half == c)
                def _():
                    j = slot(o, f)
                    cp = copy(blk(wg, j), blk(wg, j), w_snd.at[d, j], w_rcv.at[j], to)
                    cp.wait_recv()
                    if s + 1 <= hops:
                        cp.start()

    gather_step(1)
    relay = copy(tblk(a_across), tblk(a_across), tg_snd.at[2], tg_rcv.at[a_across], mate)
    relay.wait_recv()
    relay.start()
    rep_step(0)
    gather_step(2)
    rep_step(1)
    gather_step(3)
    rep_step(2)

    for k, to in ((a_mate, mate), (a_diag, mate)):
        copy(tblk(k), tblk(k), tg_snd.at[1], tg_rcv.at[k], to).wait_recv()
    for k, to in ((a_mate, mate), (a_across, across), (a_diag, diag)):
        copy(nown.at[k], nblk(k), n_snd.at[k], n_rcv.at[k], to).wait_recv()
    mt = quarter // 3 if quarter % 384 == 0 else quarter
    nt = 256
    for i in range(quarter // mt):
        nT[i * mt : (i + 1) * mt, :] = nrm[:, i * mt : (i + 1) * mt].T
    for i in range(quarter // mt):
        for n in range(hidden // nt):
            G[i * mt : (i + 1) * mt, n * nt : (n + 1) * nt] = jnp.dot(
                nT[i * mt : (i + 1) * mt, :], tg[:, n * nt : (n + 1) * nt], preferred_element_type=f32
            )

    def rs_ways(f):
        return ((1, half - f, dn, rsA, rsA_rcv), (-1, half - 1 + f, up, rsB, rsB_rcv))

    def reduce_step(s):
        for f in (1, 0):
            for sign, hops, to, buf, sem in rs_ways(f):
                if s > hops:
                    continue
                o = lax.rem(y - sign * s + n_y, n_y)

                @pl.when(o // half == c)
                def _():
                    j = slot(o, f)
                    cp = copy(blk(rsout, j), blk(buf, j), rs_snd.at[j], sem.at[j], to)
                    if s < hops:
                        cp.wait_recv()
                        rsout[ds_blk(j), :] = (G[ds_blk(j), :] + buf[ds_blk(j), :].astype(f32)).astype(bf16)
                    else:
                        rsout[ds_blk(j), :] = G[ds_blk(j), :].astype(bf16)
                    cp.start()

    reduce_step(4)
    gather_step(4)
    rep_step(3)

    def d_part(base):
        r = tok_ds(base, 2)
        for i in range(quarter // mt):
            v = lax.dot_general(
                tg[r, :], wg[i * mt : (i + 1) * mt, :], (((1,), (1,)), ((), ())), preferred_element_type=f32
            )
            dout[r, i * mt : (i + 1) * mt] = (v * (1.0 / math.sqrt(hidden))).astype(bf16)

    def d_copy(k, to):
        return copy(dout.at[tok_ds(k), :], din.at[a], d_snd.at[k], d_rcv.at[a], to)

    d_part((1 - xl) * 2)
    d_copy(a_across, across).start()
    d_copy(a_diag, diag).start()
    reduce_step(3)
    d_part(xl * 2)
    d_copy(a_mate, mate).start()
    din[a] = dout[tok_ds(a), :]
    reduce_step(2)
    reduce_step(1)

    for k, to in ((a_mate, mate), (a_across, across), (a_diag, diag)):
        copy(dout.at[tok_ds(a), :], din.at[k], d_snd.at[k], d_rcv.at[k], to).wait_recv()

    def grad_rows(i, _):
        r = pl.ds(pl.multiple_of(i * step, step), step)
        sc = scale_ref[r, :]
        total = jnp.zeros((step, 1), f32)
        for k in range(4):
            u = x_ref[r, k * quarter : (k + 1) * quarter].astype(f32) * sc
            total += jnp.sum(din[k, r, :].astype(f32) * u, axis=-1, keepdims=True)
        mean = total * (1.0 / width)
        for k in range(4):
            u = x_ref[r, k * quarter : (k + 1) * quarter].astype(f32) * sc
            ig_ref[r, k * quarter : (k + 1) * quarter] = (sc * (din[k, r, :].astype(f32) - u * mean)).astype(bf16)
        return 0

    lax.fori_loop(0, tok // step, grad_rows, 0)

    mean_delta = racc[len(masks)] / n_rep
    new_m = momentum_decay * mom_ref[...] + mean_delta
    new_g = gw_ref[...] - outer_rate * (mean_delta + momentum_decay * new_m)
    nm_ref[...] = new_m
    ng_ref[...] = new_g

    def tot_copy():
        return copy(gsend, gtot, tot_snd, tot_rcv, mate)

    @pl.when(origin)
    def _():
        for j, out in ((j1, gsend), (j0, gtot)):
            copy(blk(rsout, j), blk(rsA, j), rs_snd.at[j], rsA_rcv.at[j], dn).wait_recv()
            copy(blk(rsout, j), blk(rsB, j), rs_snd.at[j], rsB_rcv.at[j], up).wait_recv()
            r = ds_blk(j)
            out[...] = G[r, :] + rsA[r, :].astype(f32) + rsB[r, :].astype(f32)
            if out is gsend:
                tot_copy().start()
        tot_copy().wait_send()

    @pl.when(jnp.logical_not(origin))
    def _():
        tot_copy().wait_recv()

    for k in range(hidden // 128):
        cols = slice(k * 128, (k + 1) * 128)
        inner = lw_ref[:, cols] - (inner_rate * gtot[:, cols]) * (1.0 / math.sqrt(tokens_all))
        blended = blend_keep * inner + (1.0 - blend_keep) * new_g
        nl_ref[:, cols] = jnp.where(picked == k, blended, inner)

    @pl.when(origin)
    def _():
        for j in (j0, j1):
            for d, to in ((0, up), (1, dn)):
                copy(blk(wg, j), blk(wg, j), w_snd.at[d, j], w_rcv.at[j], to).wait_send()

    @pl.when(jnp.logical_not(origin))
    def _():
        copy(wown, blk(wg, jm), wp_snd, w_rcv.at[jm], mate).wait_send()

    for s in range(1, half + 1):
        for f in (0, 1):
            for sign, hops, to, d in ways(f):
                o = lax.rem(y - sign * s + n_y, n_y)
                if s <= hops:

                    @pl.when(o // half == c)
                    def _():
                        j = slot(o, f)
                        if s + 1 <= hops:
                            copy(blk(wg, j), blk(wg, j), w_snd.at[d, j], w_rcv.at[j], to).wait_send()
                        copy(blk(rsout, j), blk(rsA, j), rs_snd.at[j], rsA_rcv.at[j], dn).wait_send()

    for i in range(3):
        copy(tblk(a), tblk(a), tg_snd.at[i], tg_rcv.at[a], mate).wait_send()
    for cp in n_copies:
        cp.wait_send()
    for k, to in ((a_across, across), (a_diag, diag), (a_mate, mate)):
        d_copy(k, to).wait_send()
    for i in range(len(masks)):
        r_copy(i).wait_send()


def solution(mesh):
    n_rep, n_fsdp = mesh.shape["rep"], mesh.shape["fsdp"]
    n_y = n_fsdp // 4

    def shards(inputs, targets, local_weights, global_weights, momentum, fragment):
        x, t, lw = inputs[0], targets[0], local_weights[0]
        tok, width = x.shape
        rows, hidden = lw.shape
        quarter = width // 4
        n_masks = max(n_rep.bit_length() - 1, 1)
        vmem = pl.BlockSpec(memory_space=pltpu.VMEM)
        dma = pltpu.SemaphoreType.DMA
        V = pltpu.VMEM
        outs = pl.pallas_call(
            functools.partial(kernel, n_rep, n_y, tok * n_fsdp),
            out_shape=(
                jax.ShapeDtypeStruct((rows, hidden), f32),
                jax.ShapeDtypeStruct((tok, width), bf16),
                jax.ShapeDtypeStruct(global_weights.shape, f32),
                jax.ShapeDtypeStruct(global_weights.shape, f32),
            ),
            in_specs=[pl.BlockSpec(memory_space=pltpu.SMEM)] + [vmem] * 5,
            out_specs=(vmem,) * 4,
            scratch_shapes=[
                V((rows, hidden), bf16),
                V((quarter, hidden), bf16),
                V((4 * tok, hidden), bf16),
                V((4, tok, quarter), bf16),
                V((4 * tok, quarter), bf16),
                V((quarter, 4 * tok), bf16),
                V((quarter, hidden), f32),
                V((4 * tok, quarter), bf16),
                V((4, tok, quarter), bf16),
                V((quarter, hidden), bf16),
                V((quarter, hidden), bf16),
                V((quarter, hidden), bf16),
                V((rows, hidden), f32),
                V((rows, hidden), f32),
                V((tok, 1), f32),
                V((n_masks + 1,) + global_weights.shape, f32),
                V((n_masks,) + global_weights.shape, f32),
                dma((2, 8)), dma((8,)), dma(()),
                dma((3,)), dma((4,)),
                dma((4,)), dma((4,)),
                dma((4,)), dma((4,)),
                dma((8,)), dma((8,)), dma((8,)),
                dma(()), dma(()),
                dma((n_masks,)), dma((n_masks,)),
            ],
            compiler_params=pltpu.CompilerParams(
                collective_id=0, has_side_effects=True, vmem_limit_bytes=48 * 1024 * 1024
            ),
        )(fragment, x, t, lw, global_weights, momentum)
        new_local, input_grad, new_m, new_g = outs
        return new_local[None], input_grad[None], new_m, new_g

    placed = (
        P("rep", "fsdp", None),
        P("rep", "fsdp", None),
        P("rep", "fsdp", None),
        P("fsdp", None),
        P("fsdp", None),
        P(),
    )
    return jax.shard_map(
        shards,
        mesh=mesh,
        in_specs=placed,
        out_specs=(
            P("rep", "fsdp", None),
            P("rep", "fsdp", None),
            P("fsdp", None),
            P("fsdp", None),
        ),
        check_vma=False,
    )
```

```python
import functools
import math

import jax
import jax.numpy as jnp
from jax import lax
from jax.experimental import pallas as pl
from jax.experimental.pallas import tpu as pltpu
from jax.sharding import PartitionSpec as P

MESH = pl.DeviceIdType.MESH
bf16 = jnp.bfloat16
f32 = jnp.float32

inner_rate = 0.2
outer_rate = 0.7
momentum_decay = 0.9
blend_keep = 0.5


def kernel(
    n_rep, n_y, tokens_all,
    frag_ref, x_hbm, t_hbm, lw_hbm, gw_hbm, mom_hbm,
    nl_out, ig_out, nm_out, ng_out,
    nl_ref, ig_ref, nm_ref, ng_ref, x_ref, lw_ref, gw_ref, mom_ref, wg, tg, xT, nown, nT, G, dout, din, rsA, rsB, rsout, igT, racc, rin,
    in_sem, out_sem, w_snd, w_rcv, tg_snd, tg_rcv, n_snd, n_rcv, d_snd, d_rcv, rs_snd, rsA_rcv, rsB_rcv, r_snd, r_rcv,
):
    rep = lax.axis_index("rep")
    me = lax.axis_index("fsdp")
    half = n_y // 2
    c = lax.rem(me, 2)
    y = lax.rem(me // 2, n_y)
    xl = me // (2 * n_y)
    a = xl * 2 + c
    rows, hidden = lw_ref.shape
    tok, width = x_ref.shape
    cut = (rows // 16 + 1) // 2 * 16
    parts = ((0, cut), (cut, rows - cut))

    def dev(x_, y_, c_):
        return x_ * (2 * n_y) + y_ * 2 + c_

    def wrap(v):
        return lax.rem(v + n_y, n_y)

    up = dev(xl, wrap(y + 1), c)
    dn = dev(xl, wrap(y - 1), c)
    mate = dev(xl, y, 1 - c)
    across = dev(1 - xl, y, c)
    diag = dev(1 - xl, y, 1 - c)
    a_mate, a_across, a_diag = xl * 2 + 1 - c, (1 - xl) * 2 + c, (1 - xl) * 2 + 1 - c

    masks = []
    m = 1
    while m < n_rep:
        masks.append(m)
        m *= 2
    rep_peers = [rep + m * (1 - 2 * lax.rem(rep // m, 2)) for m in masks]

    def copy(src, dst, ss, rs, to, r=None):
        return pltpu.make_async_remote_copy(
            src_ref=src, dst_ref=dst, send_sem=ss, recv_sem=rs,
            device_id=(rep if r is None else r, to), device_id_type=MESH,
        )

    def rows_of(j, f=None):
        first, n = (0, rows) if f is None else parts[f]
        return pl.ds(pl.multiple_of(j * rows + first, 16), n)

    loads = [
        pltpu.make_async_copy(src, dst, in_sem.at[i])
        for i, (src, dst) in enumerate(
            ((lw_hbm, lw_ref), (t_hbm, tg.at[a]), (x_hbm, x_ref), (gw_hbm, gw_ref), (mom_hbm, mom_ref))
        )
    ]
    for ld in loads:
        ld.start()

    barrier = pltpu.get_barrier_semaphore()
    for peer in (up, dn, mate, across, diag):
        pl.semaphore_signal(barrier, inc=1, device_id=(rep, peer), device_id_type=MESH)
    for peer in rep_peers:
        pl.semaphore_signal(barrier, inc=1, device_id=(peer, me), device_id_type=MESH)

    loads[0].wait()
    wg[rows_of(y), :] = lw_ref[...].astype(bf16)
    pl.semaphore_wait(barrier, 5 + len(rep_peers))

    flows = ((1, 0, half, up, 0), (-1, 1, half, dn, 1), (1, 1, half - 1, up, 0), (-1, 0, half - 1, dn, 1))

    def w_copy(o, f, to, d):
        blk = wg.at[rows_of(o, f), :]
        return copy(blk, blk, w_snd.at[d, o, f], w_rcv.at[o, f], to)

    for _, f, _, to, d in flows:
        w_copy(y, f, to, d).start()

    def gather_step(s):
        for sign, f, hops, to, d in flows:
            if s <= hops:
                cp = w_copy(wrap(y - sign * s), f, to, d)
                cp.wait_recv()
                if s + 1 <= hops:
                    cp.start()

    def t_copy(k, i, to):
        return copy(tg.at[k], tg.at[k], tg_snd.at[i], tg_rcv.at[k], to)

    loads[1].wait()
    t_copy(a, 0, across).start()
    t_copy(a, 1, mate).start()

    loads[2].wait()
    tile = 128
    total = jnp.zeros((1, tok), f32)
    for i in range(width // tile):
        v = x_ref[:, i * tile : (i + 1) * tile].T
        xT[i * tile : (i + 1) * tile, :] = v
        v = v.astype(f32)
        total += jnp.sum(v * v, axis=0, keepdims=True)
    scale = lax.rsqrt(total * (1.0 / width) + 1e-06)
    n_blocks = width // rows

    def place(p):
        return 2 * (p // (2 * n_y)) + p % 2, p // 2 % n_y

    for p in range(n_blocks):
        k, j = place(p)
        u = xT[p * rows : (p + 1) * rows, :].astype(f32) * scale
        nown[k, j * rows : (j + 1) * rows, :] = u.astype(bf16)

    plane = ((a_across, across), (a_diag, diag), (a_mate, mate))

    def n_copy(k, to):
        return copy(nown.at[k], nT.at[a], n_snd.at[k], n_rcv.at[a], to)

    for k, to in plane:
        n_copy(k, to).start()
    nT[a] = nown[a]

    loads[3].wait()
    loads[4].wait()
    picked = jnp.full((rows, 128), lax.rem(frag_ref[0], hidden // 128), jnp.int32)
    frag_local = lw_ref[:, :128]
    for k in range(1, hidden // 128):
        frag_local = jnp.where(picked == k, lw_ref[:, k * 128 : (k + 1) * 128], frag_local)
    racc[0] = gw_ref[...] - frag_local

    def r_copy(i):
        return copy(racc.at[i], rin.at[i], r_snd.at[i], r_rcv.at[i], me, rep_peers[i])

    r_copy(0).start()

    def rep_step(i):
        if i < len(masks):
            r_copy(i).wait_recv()
            racc[i + 1] = racc[i] + rin[i]
            if i + 1 < len(masks):
                r_copy(i + 1).start()

    def d_block(j):
        r = rows_of(j)
        v = lax.dot_general(
            wg[r, :], tg[...].reshape(4 * tok, hidden), (((1,), (1,)), ((), ())), preferred_element_type=f32
        )
        v = (v * (1.0 / math.sqrt(hidden))).astype(bf16)
        for k in range(4):
            dout[k, r, :] = v[:, k * tok : (k + 1) * tok]

    def g_block(j):
        r = rows_of(j)
        lhs = jnp.concatenate([nT[k, r, :] for k in range(4)], axis=1)
        wide = hidden // 2
        for n in range(2):
            cols = slice(n * wide, (n + 1) * wide)
            G[r, cols] = jnp.dot(lhs, tg[:, :, cols].reshape(4 * tok, wide), preferred_element_type=f32)

    def rs_copy(o, f, sign):
        buf, sem, to = (rsA, rsA_rcv, dn) if sign == 1 else (rsB, rsB_rcv, up)
        r = rows_of(o, f)
        return copy(rsout.at[r, :], buf.at[r, :], rs_snd.at[o, f], sem.at[o, f], to)

    def reduce_part(s, sign, f):
        hops = half if (sign == 1) == (f == 0) else half - 1
        o = wrap(y - sign * s)
        r = rows_of(o, f)
        cp = rs_copy(o, f, sign)
        if s < hops:
            cp.wait_recv()
            buf = rsA if sign == 1 else rsB
            rsout[r, :] = (G[r, :] + buf[r, :].astype(f32)).astype(bf16)
        else:
            rsout[r, :] = G[r, :].astype(bf16)
        cp.start()

    gather_step(1)
    relay = t_copy(a_across, 2, mate)
    relay.wait_recv()
    relay.start()
    gather_step(2)
    rep_step(0)
    for k in (a_mate, a_diag):
        t_copy(k, 1, mate).wait_recv()
    near = [wrap(y + s) for s in (0, 1, -1, 2, -2)]
    for j in near:
        d_block(j)
    gather_step(3)
    rep_step(1)
    for k, to in ((a_mate, mate), (a_across, across), (a_diag, diag)):
        copy(nown.at[k], nT.at[k], n_snd.at[k], n_rcv.at[k], to).wait_recv()
    far = wrap(y + half)
    g_block(far)
    reduce_part(4, 1, 0)
    reduce_part(4, -1, 1)
    for sign, f in ((1, 1), (-1, 0)):
        g_block(wrap(y - sign * 3))
        reduce_part(3, sign, f)
    d_block(wrap(y + 3))
    d_block(wrap(y - 3))
    gather_step(4)
    d_block(far)

    def d_copy(k, to):
        return copy(dout.at[k], din.at[a], d_snd.at[k], d_rcv.at[a], to)

    for k, to in plane:
        d_copy(k, to).start()
    din[a] = dout[a]
    rep_step(2)
    for s in (-2, 2, -1, 1, 0):
        g_block(wrap(y + s))
    for sign, f in ((1, 0), (-1, 1)):
        reduce_part(3, sign, f)
    for s in (2, 1):
        for sign, f in ((1, 1), (-1, 0), (1, 0), (-1, 1)):
            reduce_part(s, sign, f)
        if s == 2:
            rep_step(3)

    for k, to in ((a_mate, mate), (a_across, across), (a_diag, diag)):
        copy(dout.at[k], din.at[k], d_snd.at[k], d_rcv.at[k], to).wait_recv()
    total = jnp.zeros((1, tok), f32)
    for p in range(n_blocks):
        k, j = place(p)
        u = xT[p * rows : (p + 1) * rows, :].astype(f32) * scale
        d = din[k, j * rows : (j + 1) * rows, :].astype(f32)
        total += jnp.sum(d * u, axis=0, keepdims=True)
    mean = total * (1.0 / width)
    for p in range(n_blocks):
        k, j = place(p)
        u = xT[p * rows : (p + 1) * rows, :].astype(f32) * scale
        d = din[k, j * rows : (j + 1) * rows, :].astype(f32)
        igT[p * rows : (p + 1) * rows, :] = (scale * (d - u * mean)).astype(bf16)
    for i in range(width // tile):
        ig_ref[:, i * tile : (i + 1) * tile] = igT[i * tile : (i + 1) * tile, :].T

    outs = ((ig_ref, ig_out), (nm_ref, nm_out), (ng_ref, ng_out), (nl_ref, nl_out))
    stores = [pltpu.make_async_copy(src, dst, out_sem.at[i]) for i, (src, dst) in enumerate(outs)]
    stores[0].start()

    mean_delta = racc[len(masks)] / n_rep
    new_m = momentum_decay * mom_ref[...] + mean_delta
    nm_ref[...] = new_m
    ng_ref[...] = gw_ref[...] - outer_rate * (mean_delta + momentum_decay * new_m)
    stores[1].start()
    stores[2].start()

    for f in (1, 0):
        r = rows_of(y, f)
        own = slice(parts[f][0], sum(parts[f]))
        for sign in (1, -1):
            rs_copy(y, f, sign).wait_recv()
        for k in range(hidden // 128):
            cols = slice(k * 128, (k + 1) * 128)
            grad = G[r, cols] + rsA[r, cols].astype(f32) + rsB[r, cols].astype(f32)
            inner = lw_ref[own, cols] - (inner_rate * grad) * (1.0 / math.sqrt(tokens_all))
            blended = blend_keep * inner + (1.0 - blend_keep) * ng_ref[own, :]
            nl_ref[own, cols] = jnp.where(picked[own] == k, blended, inner)

    stores[3].start()

    for s in range(half):
        for sign, f, hops, to, d in flows:
            if s + 1 <= hops:
                w_copy(wrap(y - sign * s), f, to, d).wait_send()
    for s in range(1, n_y):
        for f in (0, 1):
            rs_copy(wrap(y + s), f, 1).wait_send()
    for i in range(3):
        t_copy(a, i, mate).wait_send()
    for k, to in plane:
        n_copy(k, to).wait_send()
        d_copy(k, to).wait_send()
    for i in range(len(masks)):
        r_copy(i).wait_send()
    for st in stores:
        st.wait()


def finish(nl_in, ig_in, nm_in, ng_in, nl_out, ig_out, nm_out, ng_out, nl_ref, ig_ref, nm_ref, ng_ref, in_sem, out_sem):
    def moves(pairs, sem):
        return [pltpu.make_async_copy(src, dst, sem.at[i]) for i, (src, dst) in enumerate(pairs)]

    held = (ig_ref, nl_ref, nm_ref, ng_ref)
    loads = moves(zip((ig_in, nl_in, nm_in, ng_in), held), in_sem)
    stores = moves(zip(held, (ig_out, nl_out, nm_out, ng_out)), out_sem)
    for ld in loads:
        ld.start()
    for ld, st in zip(loads, stores):
        ld.wait()
        st.start()
    for st in stores:
        st.wait()


def solution(mesh):
    n_rep, n_fsdp = mesh.shape["rep"], mesh.shape["fsdp"]
    n_y = n_fsdp // 4

    def shards(inputs, targets, local_weights, global_weights, momentum, fragment):
        x, t, lw = inputs[0], targets[0], local_weights[0]
        tok, width = x.shape
        rows, hidden = lw.shape
        quarter = width // 4
        small = global_weights.shape
        n_masks = max(n_rep.bit_length() - 1, 1)
        limit = 63 * 1024 * 1024
        smem = pl.BlockSpec(memory_space=pltpu.SMEM)
        hbm = pl.BlockSpec(memory_space=pltpu.HBM)
        dma = pltpu.SemaphoreType.DMA
        V = pltpu.VMEM
        shape = jax.ShapeDtypeStruct
        outs = pl.pallas_call(
            functools.partial(kernel, n_rep, n_y, tok * n_fsdp),
            out_shape=(shape((rows, hidden), f32), shape((tok, width), bf16), shape(small, f32), shape(small, f32)),
            in_specs=[smem] + [hbm] * 5,
            out_specs=(hbm,) * 4,
            scratch_shapes=[
                V((rows, hidden), f32),
                V((tok, width), bf16),
                V(small, f32),
                V(small, f32),
                V((tok, width), bf16),
                V((rows, hidden), f32),
                V(small, f32),
                V(small, f32),
                V((quarter, hidden), bf16),
                V((4, tok, hidden), bf16),
                V((width, tok), bf16),
                V((4, quarter, tok), bf16),
                V((4, quarter, tok), bf16),
                V((quarter, hidden), f32),
                V((4, quarter, tok), bf16),
                V((4, quarter, tok), bf16),
                V((quarter, hidden), bf16),
                V((quarter, hidden), bf16),
                V((quarter, hidden), bf16),
                V((width, tok), bf16),
                V((n_masks + 1,) + small, f32),
                V((n_masks,) + small, f32),
                dma((5,)), dma((4,)),
                dma((2, n_y, 2)), dma((n_y, 2)),
                dma((3,)), dma((4,)),
                dma((4,)), dma((4,)),
                dma((4,)), dma((4,)),
                dma((n_y, 2)), dma((n_y, 2)), dma((n_y, 2)),
                dma((n_masks,)), dma((n_masks,)),
            ],
            compiler_params=pltpu.CompilerParams(
                collective_id=0, has_side_effects=True, vmem_limit_bytes=limit
            ),
        )(fragment, x, t, lw, global_weights, momentum)
        new_local, input_grad, new_m, new_g = pl.pallas_call(
            finish,
            out_shape=(shape((rows, hidden), f32), shape((tok, width), bf16), shape(small, f32), shape(small, f32)),
            in_specs=[hbm] * 4,
            out_specs=(hbm,) * 4,
            scratch_shapes=[
                V((rows, hidden), f32), V((tok, width), bf16), V(small, f32), V(small, f32), dma((4,)), dma((4,))
            ],
            compiler_params=pltpu.CompilerParams(vmem_limit_bytes=limit),
        )(*outs)
        return new_local[None], input_grad[None], new_m, new_g

    placed = (
        P("rep", "fsdp", None),
        P("rep", "fsdp", None),
        P("rep", "fsdp", None),
        P("fsdp", None),
        P("fsdp", None),
        P(),
    )
    return jax.shard_map(
        shards,
        mesh=mesh,
        in_specs=placed,
        out_specs=(
            P("rep", "fsdp", None),
            P("rep", "fsdp", None),
            P("fsdp", None),
            P("fsdp", None),
        ),
        check_vma=False,
    )
```

```python
import functools
import math

import jax
import jax.numpy as jnp
from jax import lax
from jax.experimental import pallas as pl
from jax.experimental.pallas import tpu as pltpu
from jax.sharding import PartitionSpec as P

MESH = pl.DeviceIdType.MESH
bf16 = jnp.bfloat16
f32 = jnp.float32

inner_rate = 0.2
outer_rate = 0.7
momentum_decay = 0.9
blend_keep = 0.5


def kernel(
    n_rep, n_y, tokens_all,
    frag_ref, x_hbm, t_hbm, lw_hbm, gw_hbm, mom_hbm,
    nl_out, ig_out, nm_out, ng_out,
    nl_ref, ig_ref, nm_ref, ng_ref, x_ref, lw_ref, gw_ref, mom_ref, wg, tg, xT, nown, nT, G, dout, din, rsA, rsB, rsout, igT, delta, rsum, ed, zin, pair, full,
    in_sem, out_sem, w_snd, w_rcv, tg_snd, tg_rcv, n_snd, n_rcv, d_snd, d_rcv, rs_snd, rsA_rcv, rsB_rcv,
    go, e_snd, e_rcv, b_snd, b_rcv, z_snd, z_rcv, p_snd, p_rcv, f_snd, f_rcv,
):
    rep = lax.axis_index("rep")
    me = lax.axis_index("fsdp")
    half = n_y // 2
    c = lax.rem(me, 2)
    y = lax.rem(me // 2, n_y)
    xl = me // (2 * n_y)
    a = xl * 2 + c
    rows, hidden = lw_ref.shape
    tok, width = x_ref.shape
    cut = (rows // 16 + 1) // 2 * 16
    parts = ((0, cut), (cut, rows - cut))

    def dev(x_, y_, c_):
        return x_ * (2 * n_y) + y_ * 2 + c_

    def wrap(v):
        return lax.rem(v + n_y, n_y)

    up = dev(xl, wrap(y + 1), c)
    dn = dev(xl, wrap(y - 1), c)
    mate = dev(xl, y, 1 - c)
    across = dev(1 - xl, y, c)
    diag = dev(1 - xl, y, 1 - c)
    a_mate, a_across, a_diag = xl * 2 + 1 - c, (1 - xl) * 2 + c, (1 - xl) * 2 + 1 - c

    n_z = n_rep // 2
    z = lax.rem(rep, n_z)
    x_peer = (1 - rep // n_z) * n_z + z

    def z_peer(t):
        zt = lax.rem(z + t, n_z)
        return zt, rep // n_z * n_z + zt

    def copy(src, dst, ss, rs, to, r=None):
        return pltpu.make_async_remote_copy(
            src_ref=src, dst_ref=dst, send_sem=ss, recv_sem=rs,
            device_id=(rep if r is None else r, to), device_id_type=MESH,
        )

    def rows_of(j, f=None):
        first, n = (0, rows) if f is None else parts[f]
        return pl.ds(pl.multiple_of(j * rows + first, 16), n)

    loads = [
        pltpu.make_async_copy(src, dst, in_sem.at[i])
        for i, (src, dst) in enumerate(
            ((lw_hbm, lw_ref), (t_hbm, tg.at[a]), (x_hbm, x_ref), (gw_hbm, gw_ref), (mom_hbm, mom_ref))
        )
    ]
    for ld in loads:
        ld.start()

    is_guide = a == 1
    is_summer = a == 3
    guide = dev(0, y, 1)
    summer = dev(1, y, 1)
    barrier = pltpu.get_barrier_semaphore()

    def tell(sem, to, r=None):
        pl.semaphore_signal(sem, inc=1, device_id=(rep if r is None else r, to), device_id_type=MESH)

    @pl.when(a != 3)
    def _():
        tell(barrier, up)
        tell(barrier, dn)

    @pl.when(a != 1)
    def _():
        tell(barrier, guide)

    @pl.when(is_summer)
    def _():
        tell(barrier, dev(0, wrap(y + 1), 1))
        tell(barrier, dev(0, wrap(y - 1), 1))
        tell(barrier, me, x_peer)
        for t in range(1, n_z):
            tell(barrier, me, z_peer(t)[1])

    loads[0].wait()
    wg[rows_of(y), :] = lw_ref[...].astype(bf16)

    @pl.when(c == 0)
    def _():
        pl.semaphore_wait(barrier, 2)

    @pl.when(is_guide)
    def _():
        pl.semaphore_wait(barrier, 7)
        for to in (dev(1, y, 1), dev(0, y, 0), dev(1, y, 0)):
            tell(go, to)

    @pl.when(is_summer)
    def _():
        pl.semaphore_wait(go, 1)

    flows = ((1, 0, half, up, 0), (-1, 1, half, dn, 1), (1, 1, half - 1, up, 0), (-1, 0, half - 1, dn, 1))

    def w_copy(o, f, to, d):
        blk = wg.at[rows_of(o, f), :]
        return copy(blk, blk, w_snd.at[d, o, f], w_rcv.at[o, f], to)

    for _, f, _, to, d in flows:
        w_copy(y, f, to, d).start()

    def gather_step(s):
        for sign, f, hops, to, d in flows:
            if s <= hops:
                cp = w_copy(wrap(y - sign * s), f, to, d)
                cp.wait_recv()
                if s + 1 <= hops:
                    cp.start()

    def t_copy(k, i, to):
        return copy(tg.at[k], tg.at[k], tg_snd.at[i], tg_rcv.at[k], to)

    def t_send():
        t_copy(a, 0, across).start()
        t_copy(a, 1, mate).start()

    loads[1].wait()
    pl.when(c == 1)(t_send)

    loads[2].wait()
    tile = 128
    total = jnp.zeros((1, tok), f32)
    for i in range(width // tile):
        v = x_ref[:, i * tile : (i + 1) * tile].T
        xT[i * tile : (i + 1) * tile, :] = v
        v = v.astype(f32)
        total += jnp.sum(v * v, axis=0, keepdims=True)
    scale = lax.rsqrt(total * (1.0 / width) + 1e-06)
    n_blocks = width // rows

    def place(p):
        return 2 * (p // (2 * n_y)) + p % 2, p // 2 % n_y

    for p in range(n_blocks):
        k, j = place(p)
        u = xT[p * rows : (p + 1) * rows, :].astype(f32) * scale
        nown[k, j * rows : (j + 1) * rows, :] = u.astype(bf16)

    plane = ((a_across, across), (a_diag, diag), (a_mate, mate))

    def n_copy(k, to):
        return copy(nown.at[k], nT.at[a], n_snd.at[k], n_rcv.at[a], to)

    loads[3].wait()
    loads[4].wait()
    picked = jnp.full((rows, 128), lax.rem(frag_ref[0], hidden // 128), jnp.int32)
    frag_local = lw_ref[:, :128]
    for k in range(1, hidden // 128):
        frag_local = jnp.where(picked == k, lw_ref[:, k * 128 : (k + 1) * 128], frag_local)
    delta[...] = gw_ref[...] - frag_local

    def e_copy(k):
        return copy(delta, ed.at[pl.ds(pl.multiple_of(k * rows, 8), rows), :], e_snd, e_rcv.at[k], summer)

    def b_copy(k, to):
        return copy(full.at[pl.ds(pl.multiple_of(k * rows, 8), rows), :], rsum, b_snd.at[k], b_rcv, to)

    @pl.when(c == 0)
    def _():
        pl.semaphore_wait(go, 1)
        t_send()

    @pl.when(a != 3)
    def _():
        e_copy(a).start()

    for k, to in plane:
        n_copy(k, to).start()
    nT[a] = nown[a]

    piece = 4 * rows // n_z
    others = ((0, dev(0, y, 0)), (1, dev(0, y, 1)), (2, dev(1, y, 0)))

    def piece_of(zt):
        return pl.ds(pl.multiple_of(zt * piece, 8), piece)

    def z_copy(t):
        zt, peer = z_peer(t)
        return copy(ed.at[piece_of(zt), :], zin.at[z], z_snd.at[t], z_rcv.at[z], me, peer)

    def f_copy(t):
        blk = full.at[piece_of(z), :]
        return copy(blk, blk, f_snd.at[t], f_rcv.at[z], me, z_peer(t)[1])

    def p_copy():
        return copy(pair.at[0], pair.at[1], p_snd, p_rcv, me, x_peer)

    def rep_start():
        @pl.when(is_summer)
        def _():
            ed[3 * rows :, :] = delta[...]
            for k, to in others:
                e_copy(k).wait_recv()
            pl.semaphore_wait(barrier, n_z)
            for t in range(1, n_z):
                z_copy(t).start()
            zin[z] = ed[piece_of(z), :]

    def rep_over_z():
        @pl.when(is_summer)
        def _():
            for t in range(1, n_z):
                zt, peer = z_peer(t)
                copy(zin.at[zt], zin.at[zt], z_snd.at[t], z_rcv.at[zt], me, peer).wait_recv()
            total = zin[0]
            for zt in range(1, n_z):
                total = total + zin[zt]
            pair[0] = total
            p_copy().start()

    def rep_over_x():
        @pl.when(is_summer)
        def _():
            p_copy().wait_recv()
            full[piece_of(z), :] = pair[0] + pair[1]
            for t in range(1, n_z):
                f_copy(t).start()

    def rep_end():
        @pl.when(is_summer)
        def _():
            for t in range(1, n_z):
                zt, peer = z_peer(t)
                blk = full.at[piece_of(zt), :]
                copy(blk, blk, f_snd.at[t], f_rcv.at[zt], me, peer).wait_recv()
            for k, to in others:
                b_copy(k, to).start()
            rsum[...] = full[3 * rows :, :]

    def d_block(j):
        r = rows_of(j)
        v = lax.dot_general(
            wg[r, :], tg[...].reshape(4 * tok, hidden), (((1,), (1,)), ((), ())), preferred_element_type=f32
        )
        v = (v * (1.0 / math.sqrt(hidden))).astype(bf16)
        for k in range(4):
            dout[k, r, :] = v[:, k * tok : (k + 1) * tok]

    def g_block(j):
        r = rows_of(j)
        lhs = jnp.concatenate([nT[k, r, :] for k in range(4)], axis=1)
        wide = hidden // 2
        for n in range(2):
            cols = slice(n * wide, (n + 1) * wide)
            G[r, cols] = jnp.dot(lhs, tg[:, :, cols].reshape(4 * tok, wide), preferred_element_type=f32)

    def rs_copy(o, f, sign):
        buf, sem, to = (rsA, rsA_rcv, dn) if sign == 1 else (rsB, rsB_rcv, up)
        r = rows_of(o, f)
        return copy(rsout.at[r, :], buf.at[r, :], rs_snd.at[o, f], sem.at[o, f], to)

    def reduce_part(s, sign, f):
        hops = half if (sign == 1) == (f == 0) else half - 1
        o = wrap(y - sign * s)
        r = rows_of(o, f)
        cp = rs_copy(o, f, sign)
        if s < hops:
            cp.wait_recv()
            buf = rsA if sign == 1 else rsB
            rsout[r, :] = (G[r, :] + buf[r, :].astype(f32)).astype(bf16)
        else:
            rsout[r, :] = G[r, :].astype(bf16)
        cp.start()

    gather_step(1)
    relay = t_copy(a_across, 2, mate)
    relay.wait_recv()
    relay.start()
    rep_start()
    gather_step(2)
    for k in (a_mate, a_diag):
        t_copy(k, 1, mate).wait_recv()
    near = [wrap(y + s) for s in (0, 1, -1, 2, -2)]
    for j in near:
        d_block(j)
    gather_step(3)
    rep_over_z()
    for k, to in ((a_mate, mate), (a_across, across), (a_diag, diag)):
        copy(nown.at[k], nT.at[k], n_snd.at[k], n_rcv.at[k], to).wait_recv()
    far = wrap(y + half)
    g_block(far)
    reduce_part(4, 1, 0)
    reduce_part(4, -1, 1)
    for sign, f in ((1, 1), (-1, 0)):
        g_block(wrap(y - sign * 3))
        reduce_part(3, sign, f)
    d_block(wrap(y + 3))
    d_block(wrap(y - 3))
    gather_step(4)
    d_block(far)

    def d_copy(k, to):
        return copy(dout.at[k], din.at[a], d_snd.at[k], d_rcv.at[a], to)

    for k, to in plane:
        d_copy(k, to).start()
    rep_over_x()
    din[a] = dout[a]
    for s in (-2, 2, -1, 1, 0):
        g_block(wrap(y + s))
    for sign, f in ((1, 0), (-1, 1)):
        reduce_part(3, sign, f)
    for s in (2, 1):
        for sign, f in ((1, 1), (-1, 0), (1, 0), (-1, 1)):
            reduce_part(s, sign, f)
        if s == 2:
            rep_end()

    for k, to in ((a_mate, mate), (a_across, across), (a_diag, diag)):
        copy(dout.at[k], din.at[k], d_snd.at[k], d_rcv.at[k], to).wait_recv()
    total = jnp.zeros((1, tok), f32)
    for p in range(n_blocks):
        k, j = place(p)
        u = xT[p * rows : (p + 1) * rows, :].astype(f32) * scale
        d = din[k, j * rows : (j + 1) * rows, :].astype(f32)
        total += jnp.sum(d * u, axis=0, keepdims=True)
    mean = total * (1.0 / width)
    for p in range(n_blocks):
        k, j = place(p)
        u = xT[p * rows : (p + 1) * rows, :].astype(f32) * scale
        d = din[k, j * rows : (j + 1) * rows, :].astype(f32)
        igT[p * rows : (p + 1) * rows, :] = (scale * (d - u * mean)).astype(bf16)
    for i in range(width // tile):
        ig_ref[:, i * tile : (i + 1) * tile] = igT[i * tile : (i + 1) * tile, :].T

    outs = ((ig_ref, ig_out), (nm_ref, nm_out), (ng_ref, ng_out), (nl_ref, nl_out))
    stores = [pltpu.make_async_copy(src, dst, out_sem.at[i]) for i, (src, dst) in enumerate(outs)]
    stores[0].start()

    @pl.when(a != 3)
    def _():
        b_copy(a, summer).wait_recv()

    mean_delta = rsum[...] / n_rep
    new_m = momentum_decay * mom_ref[...] + mean_delta
    nm_ref[...] = new_m
    ng_ref[...] = gw_ref[...] - outer_rate * (mean_delta + momentum_decay * new_m)
    stores[1].start()
    stores[2].start()

    for f in (1, 0):
        r = rows_of(y, f)
        own = slice(parts[f][0], sum(parts[f]))
        for sign in (1, -1):
            rs_copy(y, f, sign).wait_recv()
        for k in range(hidden // 128):
            cols = slice(k * 128, (k + 1) * 128)
            grad = G[r, cols] + rsA[r, cols].astype(f32) + rsB[r, cols].astype(f32)
            inner = lw_ref[own, cols] - (inner_rate * grad) * (1.0 / math.sqrt(tokens_all))
            blended = blend_keep * inner + (1.0 - blend_keep) * ng_ref[own, :]
            nl_ref[own, cols] = jnp.where(picked[own] == k, blended, inner)

    stores[3].start()

    for s in range(half):
        for sign, f, hops, to, d in flows:
            if s + 1 <= hops:
                w_copy(wrap(y - sign * s), f, to, d).wait_send()
    for s in range(1, n_y):
        for f in (0, 1):
            rs_copy(wrap(y + s), f, 1).wait_send()
    for i in range(3):
        t_copy(a, i, mate).wait_send()
    for k, to in plane:
        n_copy(k, to).wait_send()
        d_copy(k, to).wait_send()
    @pl.when(a != 3)
    def _():
        e_copy(a).wait_send()

    @pl.when(is_summer)
    def _():
        p_copy().wait_send()
        for t in range(1, n_z):
            z_copy(t).wait_send()
            f_copy(t).wait_send()
        for k, to in others:
            b_copy(k, to).wait_send()

    for st in stores:
        st.wait()


def finish(nl_in, ig_in, nm_in, ng_in, nl_out, ig_out, nm_out, ng_out, nl_ref, ig_ref, nm_ref, ng_ref, in_sem, out_sem):
    def moves(pairs, sem):
        return [pltpu.make_async_copy(src, dst, sem.at[i]) for i, (src, dst) in enumerate(pairs)]

    held = (ig_ref, nl_ref, nm_ref, ng_ref)
    loads = moves(zip((ig_in, nl_in, nm_in, ng_in), held), in_sem)
    stores = moves(zip(held, (ig_out, nl_out, nm_out, ng_out)), out_sem)
    for ld in loads:
        ld.start()
    for ld, st in zip(loads, stores):
        ld.wait()
        st.start()
    for st in stores:
        st.wait()


def solution(mesh):
    n_rep, n_fsdp = mesh.shape["rep"], mesh.shape["fsdp"]
    n_y = n_fsdp // 4

    def shards(inputs, targets, local_weights, global_weights, momentum, fragment):
        x, t, lw = inputs[0], targets[0], local_weights[0]
        tok, width = x.shape
        rows, hidden = lw.shape
        quarter = width // 4
        small = global_weights.shape
        n_z = n_rep // 2
        limit = 63 * 1024 * 1024
        smem = pl.BlockSpec(memory_space=pltpu.SMEM)
        hbm = pl.BlockSpec(memory_space=pltpu.HBM)
        dma = pltpu.SemaphoreType.DMA
        V = pltpu.VMEM
        shape = jax.ShapeDtypeStruct
        outs = pl.pallas_call(
            functools.partial(kernel, n_rep, n_y, tok * n_fsdp),
            out_shape=(shape((rows, hidden), f32), shape((tok, width), bf16), shape(small, f32), shape(small, f32)),
            in_specs=[smem] + [hbm] * 5,
            out_specs=(hbm,) * 4,
            scratch_shapes=[
                V((rows, hidden), f32),
                V((tok, width), bf16),
                V(small, f32),
                V(small, f32),
                V((tok, width), bf16),
                V((rows, hidden), f32),
                V(small, f32),
                V(small, f32),
                V((quarter, hidden), bf16),
                V((4, tok, hidden), bf16),
                V((width, tok), bf16),
                V((4, quarter, tok), bf16),
                V((4, quarter, tok), bf16),
                V((quarter, hidden), f32),
                V((4, quarter, tok), bf16),
                V((4, quarter, tok), bf16),
                V((quarter, hidden), bf16),
                V((quarter, hidden), bf16),
                V((quarter, hidden), bf16),
                V((width, tok), bf16),
                V(small, f32),
                V(small, f32),
                V((4 * rows, small[1]), f32),
                V((n_z, 4 * rows // n_z, small[1]), f32),
                V((2, 4 * rows // n_z, small[1]), f32),
                V((4 * rows, small[1]), f32),
                dma((5,)), dma((4,)),
                dma((2, n_y, 2)), dma((n_y, 2)),
                dma((3,)), dma((4,)),
                dma((4,)), dma((4,)),
                dma((4,)), dma((4,)),
                dma((n_y, 2)), dma((n_y, 2)), dma((n_y, 2)),
                pltpu.SemaphoreType.REGULAR,
                dma(()), dma((4,)), dma((4,)), dma(()),
                dma((n_z,)), dma((n_z,)), dma(()), dma(()), dma((n_z,)), dma((n_z,)),
            ],
            compiler_params=pltpu.CompilerParams(
                collective_id=0, has_side_effects=True, vmem_limit_bytes=limit
            ),
        )(fragment, x, t, lw, global_weights, momentum)
        new_local, input_grad, new_m, new_g = pl.pallas_call(
            finish,
            out_shape=(shape((rows, hidden), f32), shape((tok, width), bf16), shape(small, f32), shape(small, f32)),
            in_specs=[hbm] * 4,
            out_specs=(hbm,) * 4,
            scratch_shapes=[
                V((rows, hidden), f32), V((tok, width), bf16), V(small, f32), V(small, f32), dma((4,)), dma((4,))
            ],
            compiler_params=pltpu.CompilerParams(vmem_limit_bytes=limit),
        )(*outs)
        return new_local[None], input_grad[None], new_m, new_g

    placed = (
        P("rep", "fsdp", None),
        P("rep", "fsdp", None),
        P("rep", "fsdp", None),
        P("fsdp", None),
        P("fsdp", None),
        P(),
    )
    return jax.shard_map(
        shards,
        mesh=mesh,
        in_specs=placed,
        out_specs=(
            P("rep", "fsdp", None),
            P("rep", "fsdp", None),
            P("fsdp", None),
            P("fsdp", None),
        ),
        check_vma=False,
    )
```

```python
import functools
import math

import jax
import jax.numpy as jnp
from jax import lax
from jax.experimental import pallas as pl
from jax.experimental.pallas import tpu as pltpu
from jax.sharding import PartitionSpec as P

MESH = pl.DeviceIdType.MESH
bf16 = jnp.bfloat16
f32 = jnp.float32

inner_rate = 0.2
outer_rate = 0.7
momentum_decay = 0.9
blend_keep = 0.5


def kernel(
    n_rep, n_y, tokens_all, n_parts,
    frag_ref, x_hbm, t_hbm, lw_hbm, gw_hbm, mom_hbm,
    nl_out, ig_out, nm_out, ng_out,
    nl_ref, ig_ref, nm_ref, ng_ref, x_ref, lw_ref, gw_ref, mom_ref, wg, tg, xT, nown, nT, G, dout, din, rsA, rsB, rsout, igT, delta, rsum, ed, zin, pair, full,
    in_sem, out_sem, w_snd, w_rcv, tg_snd, tg_rcv, n_snd, n_rcv, d_snd, d_rcv, rs_snd, rsA_rcv, rsB_rcv,
    go, e_snd, e_rcv, b_snd, b_rcv, z_snd, z_rcv, p_snd, p_rcv, f_snd, f_rcv,
):
    rep = lax.axis_index("rep")
    me = lax.axis_index("fsdp")
    half = n_y // 2
    c = lax.rem(me, 2)
    y = lax.rem(me // 2, n_y)
    xl = me // (2 * n_y)
    a = xl * 2 + c
    rows, hidden = lw_ref.shape
    tok, width = x_ref.shape
    units, parts, first = rows // 16, [], 0
    for f in range(n_parts):
        n = 16 * (units // n_parts + (f < units % n_parts))
        parts.append((first, n, 1 - 2 * (f % 2)))
        first += n

    def dev(x_, y_, c_):
        return x_ * (2 * n_y) + y_ * 2 + c_

    def wrap(v):
        return lax.rem(v + n_y, n_y)

    turn = 1 - 2 * c
    up = dev(xl, wrap(y + turn), c)
    dn = dev(xl, wrap(y - turn), c)
    mate = dev(xl, y, 1 - c)
    across = dev(1 - xl, y, c)
    diag = dev(1 - xl, y, 1 - c)
    a_mate, a_across, a_diag = xl * 2 + 1 - c, (1 - xl) * 2 + c, (1 - xl) * 2 + 1 - c

    n_z = n_rep // 2
    z = lax.rem(rep, n_z)
    x_peer = (1 - rep // n_z) * n_z + z

    def z_peer(t):
        zt = lax.rem(z + t, n_z)
        return zt, rep // n_z * n_z + zt

    def copy(src, dst, ss, rs, to, r=None):
        return pltpu.make_async_remote_copy(
            src_ref=src, dst_ref=dst, send_sem=ss, recv_sem=rs,
            device_id=(rep if r is None else r, to), device_id_type=MESH,
        )

    def rows_of(j, f=None):
        first, n = (0, rows) if f is None else parts[f][:2]
        return pl.ds(pl.multiple_of(j * rows + first, 16), n)

    def load(src, dst, i):
        return pltpu.make_async_copy(src, dst, in_sem.at[i])

    w_loads = [load(lw_hbm.at[pl.ds(p[0], p[1]), :], lw_ref.at[pl.ds(p[0], p[1]), :], f) for f, p in enumerate(parts)]
    loads = [
        load(src, dst, n_parts + i)
        for i, (src, dst) in enumerate(((t_hbm, tg.at[a]), (x_hbm, x_ref), (gw_hbm, gw_ref), (mom_hbm, mom_ref)))
    ]
    for ld in w_loads:
        ld.start()

    is_guide = a == 1
    is_summer = a == 3
    guide = dev(0, y, 1)
    summer = dev(1, y, 1)
    barrier = pltpu.get_barrier_semaphore()

    def tell(sem, to, r=None):
        pl.semaphore_signal(sem, inc=1, device_id=(rep if r is None else r, to), device_id_type=MESH)

    @pl.when(a != 3)
    def _():
        tell(barrier, up)
        tell(barrier, dn)

    @pl.when(a != 1)
    def _():
        tell(barrier, guide)

    @pl.when(is_summer)
    def _():
        tell(barrier, dev(0, wrap(y + 1), 1))
        tell(barrier, dev(0, wrap(y - 1), 1))
        tell(barrier, me, x_peer)
        for t in range(1, n_z):
            tell(barrier, me, z_peer(t)[1])

    for ld in loads:
        ld.start()
    for f, p in enumerate(parts):
        w_loads[f].wait()
        wg[rows_of(y, f), :] = lw_ref[p[0] : p[0] + p[1], :].astype(bf16)

    @pl.when(c == 0)
    def _():
        pl.semaphore_wait(barrier, 2)

    @pl.when(is_guide)
    def _():
        pl.semaphore_wait(barrier, 7)
        for to in (dev(1, y, 1), dev(0, y, 0), dev(1, y, 0)):
            tell(go, to)

    @pl.when(is_summer)
    def _():
        pl.semaphore_wait(go, 1)

    flows = [
        (sign, f, hops, up if sign == 1 else dn, int(sign != 1))
        for far_way, hops in ((1, half), (-1, half - 1))
        for f, sign in enumerate(far_way * p[2] for p in parts)
    ]
    long_flows, short_flows = flows[:n_parts], flows[n_parts:]

    def w_copy(o, f, to, d):
        blk = wg.at[rows_of(o, f), :]
        return copy(blk, blk, w_snd.at[d, o, f], w_rcv.at[o, f], to)

    for _, f, _, to, d in flows:
        w_copy(y, f, to, d).start()

    def gather_step(s):
        for sign, f, hops, to, d in flows:
            if s <= hops:
                cp = w_copy(wrap(y - turn * sign * s), f, to, d)
                cp.wait_recv()
                if s + 1 <= hops:
                    cp.start()

    def t_copy(k, i, to):
        return copy(tg.at[k], tg.at[k], tg_snd.at[i], tg_rcv.at[k], to)

    def t_send():
        t_copy(a, 0, across).start()
        t_copy(a, 1, mate).start()

    loads[0].wait()
    pl.when(c == 1)(t_send)

    loads[1].wait()
    tile = 128
    total = jnp.zeros((1, tok), f32)
    for i in range(width // tile):
        v = x_ref[:, i * tile : (i + 1) * tile].T
        xT[i * tile : (i + 1) * tile, :] = v
        v = v.astype(f32)
        total += jnp.sum(v * v, axis=0, keepdims=True)
    scale = lax.rsqrt(total * (1.0 / width) + 1e-06)
    n_blocks = width // rows

    def place(p):
        return 2 * (p // (2 * n_y)) + p % 2, p // 2 % n_y

    for p in range(n_blocks):
        k, j = place(p)
        u = xT[p * rows : (p + 1) * rows, :].astype(f32) * scale
        nown[k, j * rows : (j + 1) * rows, :] = u.astype(bf16)

    plane = ((a_across, across), (a_diag, diag), (a_mate, mate))

    def n_copy(k, to):
        return copy(nown.at[k], nT.at[a], n_snd.at[k], n_rcv.at[a], to)

    loads[2].wait()
    loads[3].wait()
    picked = jnp.full((rows, 128), lax.rem(frag_ref[0], hidden // 128), jnp.int32)
    frag_local = lw_ref[:, :128]
    for k in range(1, hidden // 128):
        frag_local = jnp.where(picked == k, lw_ref[:, k * 128 : (k + 1) * 128], frag_local)
    delta[...] = gw_ref[...] - frag_local

    def e_copy(k):
        return copy(delta, ed.at[pl.ds(pl.multiple_of(k * rows, 8), rows), :], e_snd, e_rcv.at[k], summer)

    def b_copy(k, to):
        return copy(full.at[pl.ds(pl.multiple_of(k * rows, 8), rows), :], rsum, b_snd.at[k], b_rcv, to)

    @pl.when(c == 0)
    def _():
        pl.semaphore_wait(go, 1)
        t_send()

    @pl.when(a != 3)
    def _():
        e_copy(a).start()

    for k, to in plane:
        n_copy(k, to).start()
    nT[a] = nown[a]

    piece = 4 * rows // n_z
    others = ((0, dev(0, y, 0)), (1, dev(0, y, 1)), (2, dev(1, y, 0)))

    def piece_of(zt):
        return pl.ds(pl.multiple_of(zt * piece, 8), piece)

    def z_copy(t):
        zt, peer = z_peer(t)
        return copy(ed.at[piece_of(zt), :], zin.at[z], z_snd.at[t], z_rcv.at[z], me, peer)

    def f_copy(t):
        blk = full.at[piece_of(z), :]
        return copy(blk, blk, f_snd.at[t], f_rcv.at[z], me, z_peer(t)[1])

    def p_copy():
        return copy(pair.at[0], pair.at[1], p_snd, p_rcv, me, x_peer)

    def rep_start():
        @pl.when(is_summer)
        def _():
            ed[3 * rows :, :] = delta[...]
            for k, to in others:
                e_copy(k).wait_recv()
            pl.semaphore_wait(barrier, n_z)
            for t in range(1, n_z):
                z_copy(t).start()
            zin[z] = ed[piece_of(z), :]

    def rep_over_z():
        @pl.when(is_summer)
        def _():
            for t in range(1, n_z):
                zt, peer = z_peer(t)
                copy(zin.at[zt], zin.at[zt], z_snd.at[t], z_rcv.at[zt], me, peer).wait_recv()
            total = zin[0]
            for zt in range(1, n_z):
                total = total + zin[zt]
            pair[0] = total
            p_copy().start()

    def rep_over_x():
        @pl.when(is_summer)
        def _():
            p_copy().wait_recv()
            full[piece_of(z), :] = pair[0] + pair[1]
            for t in range(1, n_z):
                f_copy(t).start()

    def rep_end():
        @pl.when(is_summer)
        def _():
            for t in range(1, n_z):
                zt, peer = z_peer(t)
                blk = full.at[piece_of(zt), :]
                copy(blk, blk, f_snd.at[t], f_rcv.at[zt], me, peer).wait_recv()
            for k, to in others:
                b_copy(k, to).start()
            rsum[...] = full[3 * rows :, :]

    def d_block(j):
        r = rows_of(j)
        v = lax.dot_general(
            wg[r, :], tg[...].reshape(4 * tok, hidden), (((1,), (1,)), ((), ())), preferred_element_type=f32
        )
        v = (v * (1.0 / math.sqrt(hidden))).astype(bf16)
        for k in range(4):
            dout[k, r, :] = v[:, k * tok : (k + 1) * tok]

    def g_block(j):
        r = rows_of(j)
        lhs = jnp.concatenate([nT[k, r, :] for k in range(4)], axis=1)
        wide = hidden // 2
        for n in range(2):
            cols = slice(n * wide, (n + 1) * wide)
            G[r, cols] = jnp.dot(lhs, tg[:, :, cols].reshape(4 * tok, wide), preferred_element_type=f32)

    def rs_copy(o, f, sign):
        buf, sem, to = (rsA, rsA_rcv, dn) if sign == 1 else (rsB, rsB_rcv, up)
        r = rows_of(o, f)
        return copy(rsout.at[r, :], buf.at[r, :], rs_snd.at[o, f], sem.at[o, f], to)

    def reduce_part(s, sign, f):
        hops = half if sign == parts[f][2] else half - 1
        o = wrap(y - turn * sign * s)
        r = rows_of(o, f)
        cp = rs_copy(o, f, sign)
        if s < hops:
            cp.wait_recv()
            buf = rsA if sign == 1 else rsB
            rsout[r, :] = (G[r, :] + buf[r, :].astype(f32)).astype(bf16)
        else:
            rsout[r, :] = G[r, :].astype(bf16)
        cp.start()

    gather_step(1)
    relay = t_copy(a_across, 2, mate)
    relay.wait_recv()
    relay.start()
    rep_start()
    gather_step(2)
    for k in (a_mate, a_diag):
        t_copy(k, 1, mate).wait_recv()
    near = [wrap(y + s) for s in (0, 1, -1, 2, -2)]
    for j in near:
        d_block(j)
    gather_step(3)
    rep_over_z()
    for k, to in ((a_mate, mate), (a_across, across), (a_diag, diag)):
        copy(nown.at[k], nT.at[k], n_snd.at[k], n_rcv.at[k], to).wait_recv()
    far = wrap(y + half)
    g_block(far)
    for sign, f, *_ in long_flows:
        reduce_part(half, sign, f)
    for s in (3, -3):
        g_block(wrap(y + s))
    for sign, f, *_ in short_flows:
        reduce_part(3, sign, f)
    d_block(wrap(y + 3))
    d_block(wrap(y - 3))
    gather_step(4)
    d_block(far)

    def d_copy(k, to):
        return copy(dout.at[k], din.at[a], d_snd.at[k], d_rcv.at[a], to)

    for k, to in plane:
        d_copy(k, to).start()
    rep_over_x()
    din[a] = dout[a]
    for s in (-2, 2, -1, 1, 0):
        g_block(wrap(y + s))
    for sign, f, *_ in long_flows:
        reduce_part(3, sign, f)
    for s in (2, 1):
        for sign, f, *_ in short_flows + long_flows:
            reduce_part(s, sign, f)
        if s == 2:
            rep_end()

    for k, to in ((a_mate, mate), (a_across, across), (a_diag, diag)):
        copy(dout.at[k], din.at[k], d_snd.at[k], d_rcv.at[k], to).wait_recv()
    total = jnp.zeros((1, tok), f32)
    for p in range(n_blocks):
        k, j = place(p)
        u = xT[p * rows : (p + 1) * rows, :].astype(f32) * scale
        d = din[k, j * rows : (j + 1) * rows, :].astype(f32)
        total += jnp.sum(d * u, axis=0, keepdims=True)
    mean = total * (1.0 / width)
    for p in range(n_blocks):
        k, j = place(p)
        u = xT[p * rows : (p + 1) * rows, :].astype(f32) * scale
        d = din[k, j * rows : (j + 1) * rows, :].astype(f32)
        igT[p * rows : (p + 1) * rows, :] = (scale * (d - u * mean)).astype(bf16)
    for i in range(width // tile):
        ig_ref[:, i * tile : (i + 1) * tile] = igT[i * tile : (i + 1) * tile, :].T

    outs = [(ig_ref, ig_out), (nm_ref, nm_out), (ng_ref, ng_out)]
    outs += [(nl_ref.at[pl.ds(p[0], p[1]), :], nl_out.at[pl.ds(p[0], p[1]), :]) for p in parts]
    stores = [pltpu.make_async_copy(src, dst, out_sem.at[i]) for i, (src, dst) in enumerate(outs)]
    stores[0].start()

    @pl.when(a != 3)
    def _():
        b_copy(a, summer).wait_recv()

    mean_delta = rsum[...] / n_rep
    new_m = momentum_decay * mom_ref[...] + mean_delta
    nm_ref[...] = new_m
    ng_ref[...] = gw_ref[...] - outer_rate * (mean_delta + momentum_decay * new_m)
    stores[1].start()
    stores[2].start()

    for f in range(n_parts):
        r = rows_of(y, f)
        own = slice(parts[f][0], parts[f][0] + parts[f][1])
        for sign in (1, -1):
            rs_copy(y, f, sign).wait_recv()
        for k in range(hidden // 128):
            cols = slice(k * 128, (k + 1) * 128)
            grad = G[r, cols] + rsA[r, cols].astype(f32) + rsB[r, cols].astype(f32)
            inner = lw_ref[own, cols] - (inner_rate * grad) * (1.0 / math.sqrt(tokens_all))
            blended = blend_keep * inner + (1.0 - blend_keep) * ng_ref[own, :]
            nl_ref[own, cols] = jnp.where(picked[own] == k, blended, inner)
        stores[3 + f].start()

    for s in range(half):
        for sign, f, hops, to, d in flows:
            if s + 1 <= hops:
                w_copy(wrap(y - turn * sign * s), f, to, d).wait_send()
    for s in range(1, n_y):
        for f in range(n_parts):
            rs_copy(wrap(y + s), f, 1).wait_send()
    for i in range(3):
        t_copy(a, i, mate).wait_send()
    for k, to in plane:
        n_copy(k, to).wait_send()
        d_copy(k, to).wait_send()
    @pl.when(a != 3)
    def _():
        e_copy(a).wait_send()

    @pl.when(is_summer)
    def _():
        p_copy().wait_send()
        for t in range(1, n_z):
            z_copy(t).wait_send()
            f_copy(t).wait_send()
        for k, to in others:
            b_copy(k, to).wait_send()

    for st in stores:
        st.wait()


def finish(nl_in, ig_in, nm_in, ng_in, nl_out, ig_out, nm_out, ng_out, nl_ref, ig_ref, nm_ref, ng_ref, in_sem, out_sem):
    loads, stores = [], []
    for src, held, dst, n in (
        (ig_in, ig_ref, ig_out, 4), (nl_in, nl_ref, nl_out, 3), (nm_in, nm_ref, nm_out, 1), (ng_in, ng_ref, ng_out, 1)
    ):
        n = min(n, src.shape[0] // 16)
        size = src.shape[0] // n // 16 * 16
        for i in range(n):
            part = pl.ds(i * size, size if i < n - 1 else src.shape[0] - i * size)
            at = len(loads)
            loads.append(pltpu.make_async_copy(src.at[part, :], held.at[part, :], in_sem.at[at]))
            stores.append(pltpu.make_async_copy(held.at[part, :], dst.at[part, :], out_sem.at[at]))
    for ld in loads:
        ld.start()
    for ld, st in zip(loads, stores):
        ld.wait()
        st.start()
    for st in stores:
        st.wait()


def solution(mesh):
    n_rep, n_fsdp = mesh.shape["rep"], mesh.shape["fsdp"]
    n_y = n_fsdp // 4

    def shards(inputs, targets, local_weights, global_weights, momentum, fragment):
        x, t, lw = inputs[0], targets[0], local_weights[0]
        tok, width = x.shape
        rows, hidden = lw.shape
        quarter = width // 4
        small = global_weights.shape
        n_z = n_rep // 2
        limit = 63 * 1024 * 1024
        n_parts = min(2, rows // 16)
        smem = pl.BlockSpec(memory_space=pltpu.SMEM)
        hbm = pl.BlockSpec(memory_space=pltpu.HBM)
        dma = pltpu.SemaphoreType.DMA
        V = pltpu.VMEM
        shape = jax.ShapeDtypeStruct
        outs = pl.pallas_call(
            functools.partial(kernel, n_rep, n_y, tok * n_fsdp, n_parts),
            out_shape=(shape((rows, hidden), f32), shape((tok, width), bf16), shape(small, f32), shape(small, f32)),
            in_specs=[smem] + [hbm] * 5,
            out_specs=(hbm,) * 4,
            scratch_shapes=[
                V((rows, hidden), f32),
                V((tok, width), bf16),
                V(small, f32),
                V(small, f32),
                V((tok, width), bf16),
                V((rows, hidden), f32),
                V(small, f32),
                V(small, f32),
                V((quarter, hidden), bf16),
                V((4, tok, hidden), bf16),
                V((width, tok), bf16),
                V((4, quarter, tok), bf16),
                V((4, quarter, tok), bf16),
                V((quarter, hidden), f32),
                V((4, quarter, tok), bf16),
                V((4, quarter, tok), bf16),
                V((quarter, hidden), bf16),
                V((quarter, hidden), bf16),
                V((quarter, hidden), bf16),
                V((width, tok), bf16),
                V(small, f32),
                V(small, f32),
                V((4 * rows, small[1]), f32),
                V((n_z, 4 * rows // n_z, small[1]), f32),
                V((2, 4 * rows // n_z, small[1]), f32),
                V((4 * rows, small[1]), f32),
                dma((4 + n_parts,)), dma((3 + n_parts,)),
                dma((2, n_y, n_parts)), dma((n_y, n_parts)),
                dma((3,)), dma((4,)),
                dma((4,)), dma((4,)),
                dma((4,)), dma((4,)),
                dma((n_y, n_parts)), dma((n_y, n_parts)), dma((n_y, n_parts)),
                pltpu.SemaphoreType.REGULAR,
                dma(()), dma((4,)), dma((4,)), dma(()),
                dma((n_z,)), dma((n_z,)), dma(()), dma(()), dma((n_z,)), dma((n_z,)),
            ],
            compiler_params=pltpu.CompilerParams(
                collective_id=0, has_side_effects=True, vmem_limit_bytes=limit
            ),
        )(fragment, x, t, lw, global_weights, momentum)
        new_local, input_grad, new_m, new_g = pl.pallas_call(
            finish,
            out_shape=(shape((rows, hidden), f32), shape((tok, width), bf16), shape(small, f32), shape(small, f32)),
            in_specs=[hbm] * 4,
            out_specs=(hbm,) * 4,
            scratch_shapes=[
                V((rows, hidden), f32), V((tok, width), bf16), V(small, f32), V(small, f32), dma((9,)), dma((9,))
            ],
            compiler_params=pltpu.CompilerParams(vmem_limit_bytes=limit),
        )(*outs)
        return new_local[None], input_grad[None], new_m, new_g

    placed = (
        P("rep", "fsdp", None),
        P("rep", "fsdp", None),
        P("rep", "fsdp", None),
        P("fsdp", None),
        P("fsdp", None),
        P(),
    )
    return jax.shard_map(
        shards,
        mesh=mesh,
        in_specs=placed,
        out_specs=(
            P("rep", "fsdp", None),
            P("rep", "fsdp", None),
            P("fsdp", None),
            P("fsdp", None),
        ),
        check_vma=False,
    )
```

```python
import functools
import math

import jax
import jax.numpy as jnp
from jax import lax
from jax.experimental import pallas as pl
from jax.experimental.pallas import tpu as pltpu
from jax.sharding import PartitionSpec as P

MESH = pl.DeviceIdType.MESH
bf16 = jnp.bfloat16
f32 = jnp.float32

inner_rate = 0.2
outer_rate = 0.7
momentum_decay = 0.9
blend_keep = 0.5


def kernel(
    n_rep, n_y, tokens_all, n_parts,
    frag_ref, x_hbm, t_hbm, lw_hbm, gw_hbm, mom_hbm,
    nl_out, ig_out, nm_out, ng_out,
    nl_ref, ig_ref, nm_ref, ng_ref, x_ref, lw_ref, gw_ref, mom_ref, wg, tg, xT, nown, nT, G, dout, din, rsA, rsB, rsout, igT, delta, rsum, ed, zin, pair, full,
    in_sem, out_sem, w_snd, w_rcv, tg_snd, tg_rcv, n_snd, n_rcv, d_snd, d_rcv, rs_snd, rsA_rcv, rsB_rcv,
    go, e_snd, e_rcv, b_snd, b_rcv, z_snd, z_rcv, p_snd, p_rcv, f_snd, f_rcv,
):
    rep = lax.axis_index("rep")
    me = lax.axis_index("fsdp")
    half = n_y // 2
    c = lax.rem(me, 2)
    y = lax.rem(me // 2, n_y)
    xl = me // (2 * n_y)
    a = xl * 2 + c
    rows, hidden = lw_ref.shape
    tok, width = x_ref.shape
    units, parts, first = rows // 16, [], 0
    for f in range(n_parts):
        n = 16 * (units // n_parts + (f < units % n_parts))
        parts.append((first, n, 1 - 2 * (f % 2)))
        first += n

    def dev(x_, y_, c_):
        return x_ * (2 * n_y) + y_ * 2 + c_

    def wrap(v):
        return lax.rem(v + n_y, n_y)

    turn = 1 - 2 * c
    up = dev(xl, wrap(y + turn), c)
    dn = dev(xl, wrap(y - turn), c)
    mate = dev(xl, y, 1 - c)
    across = dev(1 - xl, y, c)
    diag = dev(1 - xl, y, 1 - c)
    a_mate, a_across, a_diag = xl * 2 + 1 - c, (1 - xl) * 2 + c, (1 - xl) * 2 + 1 - c

    n_z = n_rep // 2
    z = lax.rem(rep, n_z)
    x_peer = (1 - rep // n_z) * n_z + z

    def z_peer(t):
        zt = lax.rem(z + t, n_z)
        return zt, rep // n_z * n_z + zt

    def copy(src, dst, ss, rs, to, r=None):
        return pltpu.make_async_remote_copy(
            src_ref=src, dst_ref=dst, send_sem=ss, recv_sem=rs,
            device_id=(rep if r is None else r, to), device_id_type=MESH,
        )

    def rows_of(j, f=None):
        first, n = (0, rows) if f is None else parts[f][:2]
        return pl.ds(pl.multiple_of(j * rows + first, 16), n)

    def load(src, dst, i):
        return pltpu.make_async_copy(src, dst, in_sem.at[i])

    w_loads = [load(lw_hbm.at[pl.ds(p[0], p[1]), :], lw_ref.at[pl.ds(p[0], p[1]), :], f) for f, p in enumerate(parts)]
    loads = [
        load(src, dst, n_parts + i)
        for i, (src, dst) in enumerate(((t_hbm, tg.at[a]), (x_hbm, x_ref), (gw_hbm, gw_ref), (mom_hbm, mom_ref)))
    ]
    for ld in w_loads:
        ld.start()

    is_guide = a == 1
    is_summer = a == 3
    guide = dev(0, y, 1)
    summer = dev(1, y, 1)
    barrier = pltpu.get_barrier_semaphore()

    def tell(sem, to, r=None):
        pl.semaphore_signal(sem, inc=1, device_id=(rep if r is None else r, to), device_id_type=MESH)

    @pl.when(a != 3)
    def _():
        tell(barrier, up)
        tell(barrier, dn)

    @pl.when(a != 1)
    def _():
        tell(barrier, guide)

    @pl.when(is_summer)
    def _():
        tell(barrier, dev(0, wrap(y + 1), 1))
        tell(barrier, dev(0, wrap(y - 1), 1))
        tell(barrier, me, x_peer)
        for t in range(1, n_z):
            tell(barrier, me, z_peer(t)[1])

    for ld in loads:
        ld.start()
    for f, p in enumerate(parts):
        w_loads[f].wait()
        wg[rows_of(y, f), :] = lw_ref[p[0] : p[0] + p[1], :].astype(bf16)

    @pl.when(c == 0)
    def _():
        pl.semaphore_wait(barrier, 2)

    @pl.when(is_guide)
    def _():
        pl.semaphore_wait(barrier, 7)
        for to in (dev(1, y, 1), dev(0, y, 0), dev(1, y, 0)):
            tell(go, to)

    @pl.when(is_summer)
    def _():
        pl.semaphore_wait(go, 1)

    flows = [
        (sign, f, hops, up if sign == 1 else dn, int(sign != 1))
        for far_way, hops in ((1, half), (-1, half - 1))
        for f, sign in enumerate(far_way * p[2] for p in parts)
    ]
    long_flows, short_flows = flows[:n_parts], flows[n_parts:]

    def w_copy(o, f, to, d):
        blk = wg.at[rows_of(o, f), :]
        return copy(blk, blk, w_snd.at[d, o, f], w_rcv.at[o, f], to)

    for _, f, _, to, d in flows:
        w_copy(y, f, to, d).start()

    def gather_step(s, ways=flows):
        for sign, f, hops, to, d in ways:
            if s <= hops:
                cp = w_copy(wrap(y - turn * sign * s), f, to, d)
                cp.wait_recv()
                if s + 1 <= hops:
                    cp.start()

    def t_copy(k, i, to):
        return copy(tg.at[k], tg.at[k], tg_snd.at[i], tg_rcv.at[k], to)

    def t_send():
        t_copy(a, 0, across).start()
        t_copy(a, 1, mate).start()

    loads[0].wait()
    pl.when(c == 1)(t_send)

    loads[1].wait()
    tile = 128
    total = jnp.zeros((1, tok), f32)
    for i in range(width // tile):
        v = x_ref[:, i * tile : (i + 1) * tile].T
        xT[i * tile : (i + 1) * tile, :] = v
        v = v.astype(f32)
        total += jnp.sum(v * v, axis=0, keepdims=True)
    scale = lax.rsqrt(total * (1.0 / width) + 1e-06)
    n_blocks = width // rows

    def place(p):
        return 2 * (p // (2 * n_y)) + p % 2, p // 2 % n_y

    for p in range(n_blocks):
        k, j = place(p)
        u = xT[p * rows : (p + 1) * rows, :].astype(f32) * scale
        nown[k, j * rows : (j + 1) * rows, :] = u.astype(bf16)

    plane = ((a_across, across), (a_diag, diag), (a_mate, mate))

    def n_copy(k, to):
        return copy(nown.at[k], nT.at[a], n_snd.at[k], n_rcv.at[a], to)

    gather_step(1, long_flows)

    loads[2].wait()
    loads[3].wait()
    picked = jnp.full((rows, 128), lax.rem(frag_ref[0], hidden // 128), jnp.int32)
    frag_local = lw_ref[:, :128]
    for k in range(1, hidden // 128):
        frag_local = jnp.where(picked == k, lw_ref[:, k * 128 : (k + 1) * 128], frag_local)
    delta[...] = gw_ref[...] - frag_local

    def e_copy(k):
        return copy(delta, ed.at[pl.ds(pl.multiple_of(k * rows, 8), rows), :], e_snd, e_rcv.at[k], summer)

    def b_copy(k, to):
        return copy(full.at[pl.ds(pl.multiple_of(k * rows, 8), rows), :], rsum, b_snd.at[k], b_rcv, to)

    @pl.when(c == 0)
    def _():
        pl.semaphore_wait(go, 1)
        t_send()

    @pl.when(a != 3)
    def _():
        e_copy(a).start()

    for k, to in plane:
        n_copy(k, to).start()
    nT[a] = nown[a]

    piece = 4 * rows // n_z
    others = ((0, dev(0, y, 0)), (1, dev(0, y, 1)), (2, dev(1, y, 0)))

    def piece_of(zt):
        return pl.ds(pl.multiple_of(zt * piece, 8), piece)

    def z_copy(t):
        zt, peer = z_peer(t)
        return copy(ed.at[piece_of(zt), :], zin.at[z], z_snd.at[t], z_rcv.at[z], me, peer)

    def f_copy(t):
        blk = full.at[piece_of(z), :]
        return copy(blk, blk, f_snd.at[t], f_rcv.at[z], me, z_peer(t)[1])

    def p_copy():
        return copy(pair.at[0], pair.at[1], p_snd, p_rcv, me, x_peer)

    def rep_start():
        @pl.when(is_summer)
        def _():
            ed[3 * rows :, :] = delta[...]
            for k, to in others:
                e_copy(k).wait_recv()
            pl.semaphore_wait(barrier, n_z)
            for t in range(1, n_z):
                z_copy(t).start()
            zin[z] = ed[piece_of(z), :]

    def rep_over_z():
        @pl.when(is_summer)
        def _():
            for t in range(1, n_z):
                zt, peer = z_peer(t)
                copy(zin.at[zt], zin.at[zt], z_snd.at[t], z_rcv.at[zt], me, peer).wait_recv()
            total = zin[0]
            for zt in range(1, n_z):
                total = total + zin[zt]
            pair[0] = total
            p_copy().start()

    def rep_over_x():
        @pl.when(is_summer)
        def _():
            p_copy().wait_recv()
            full[piece_of(z), :] = pair[0] + pair[1]
            for t in range(1, n_z):
                f_copy(t).start()

    def rep_end():
        @pl.when(is_summer)
        def _():
            for t in range(1, n_z):
                zt, peer = z_peer(t)
                blk = full.at[piece_of(zt), :]
                copy(blk, blk, f_snd.at[t], f_rcv.at[zt], me, peer).wait_recv()
            for k, to in others:
                b_copy(k, to).start()
            rsum[...] = full[3 * rows :, :]

    def d_block(j):
        r = rows_of(j)
        v = lax.dot_general(
            wg[r, :], tg[...].reshape(4 * tok, hidden), (((1,), (1,)), ((), ())), preferred_element_type=f32
        )
        v = (v * (1.0 / math.sqrt(hidden))).astype(bf16)
        for k in range(4):
            dout[k, r, :] = v[:, k * tok : (k + 1) * tok]

    def g_block(j):
        r = rows_of(j)
        lhs = jnp.concatenate([nT[k, r, :] for k in range(4)], axis=1)
        wide = hidden // 2
        for n in range(2):
            cols = slice(n * wide, (n + 1) * wide)
            G[r, cols] = jnp.dot(lhs, tg[:, :, cols].reshape(4 * tok, wide), preferred_element_type=f32)

    def rs_copy(o, f, sign):
        buf, sem, to = (rsA, rsA_rcv, dn) if sign == 1 else (rsB, rsB_rcv, up)
        r = rows_of(o, f)
        return copy(rsout.at[r, :], buf.at[r, :], rs_snd.at[o, f], sem.at[o, f], to)

    def reduce_part(s, sign, f):
        hops = half if sign == parts[f][2] else half - 1
        o = wrap(y - turn * sign * s)
        r = rows_of(o, f)
        cp = rs_copy(o, f, sign)
        if s < hops:
            cp.wait_recv()
            buf = rsA if sign == 1 else rsB
            rsout[r, :] = (G[r, :] + buf[r, :].astype(f32)).astype(bf16)
        else:
            rsout[r, :] = G[r, :].astype(bf16)
        cp.start()

    gather_step(1, short_flows)
    relay = t_copy(a_across, 2, mate)
    relay.wait_recv()
    relay.start()
    rep_start()
    gather_step(2)
    for k in (a_mate, a_diag):
        t_copy(k, 1, mate).wait_recv()
    near = [wrap(y + s) for s in (0, 1, -1, 2, -2)]
    for j in near:
        d_block(j)
    gather_step(3)
    rep_over_z()
    for k, to in ((a_mate, mate), (a_across, across), (a_diag, diag)):
        copy(nown.at[k], nT.at[k], n_snd.at[k], n_rcv.at[k], to).wait_recv()
    far = wrap(y + half)
    g_block(far)
    for sign, f, *_ in long_flows:
        reduce_part(half, sign, f)
    for s in (3, -3):
        g_block(wrap(y + s))
    for sign, f, *_ in short_flows:
        reduce_part(3, sign, f)
    d_block(wrap(y + 3))
    d_block(wrap(y - 3))
    gather_step(4)
    d_block(far)

    def d_copy(k, to):
        return copy(dout.at[k], din.at[a], d_snd.at[k], d_rcv.at[a], to)

    for k, to in plane:
        d_copy(k, to).start()
    rep_over_x()
    din[a] = dout[a]
    for s in (-2, 2, -1, 1, 0):
        g_block(wrap(y + s))
    for sign, f, *_ in long_flows:
        reduce_part(3, sign, f)
    for s in (2, 1):
        for sign, f, *_ in short_flows + long_flows:
            reduce_part(s, sign, f)
        if s == 2:
            rep_end()

    for k, to in ((a_mate, mate), (a_across, across), (a_diag, diag)):
        copy(dout.at[k], din.at[k], d_snd.at[k], d_rcv.at[k], to).wait_recv()
    total = jnp.zeros((1, tok), f32)
    for p in range(n_blocks):
        k, j = place(p)
        u = xT[p * rows : (p + 1) * rows, :].astype(f32) * scale
        d = din[k, j * rows : (j + 1) * rows, :].astype(f32)
        total += jnp.sum(d * u, axis=0, keepdims=True)
    mean = total * (1.0 / width)
    for p in range(n_blocks):
        k, j = place(p)
        u = xT[p * rows : (p + 1) * rows, :].astype(f32) * scale
        d = din[k, j * rows : (j + 1) * rows, :].astype(f32)
        igT[p * rows : (p + 1) * rows, :] = (scale * (d - u * mean)).astype(bf16)
    for i in range(width // tile):
        ig_ref[:, i * tile : (i + 1) * tile] = igT[i * tile : (i + 1) * tile, :].T

    outs = [(ig_ref, ig_out), (nm_ref, nm_out), (ng_ref, ng_out)]
    outs += [(nl_ref.at[pl.ds(p[0], p[1]), :], nl_out.at[pl.ds(p[0], p[1]), :]) for p in parts]
    stores = [pltpu.make_async_copy(src, dst, out_sem.at[i]) for i, (src, dst) in enumerate(outs)]
    stores[0].start()

    @pl.when(a != 3)
    def _():
        b_copy(a, summer).wait_recv()

    mean_delta = rsum[...] / n_rep
    new_m = momentum_decay * mom_ref[...] + mean_delta
    nm_ref[...] = new_m
    ng_ref[...] = gw_ref[...] - outer_rate * (mean_delta + momentum_decay * new_m)
    stores[1].start()
    stores[2].start()

    for f in range(n_parts):
        r = rows_of(y, f)
        own = slice(parts[f][0], parts[f][0] + parts[f][1])
        for sign in (1, -1):
            rs_copy(y, f, sign).wait_recv()
        for k in range(hidden // 128):
            cols = slice(k * 128, (k + 1) * 128)
            grad = G[r, cols] + rsA[r, cols].astype(f32) + rsB[r, cols].astype(f32)
            inner = lw_ref[own, cols] - (inner_rate * grad) * (1.0 / math.sqrt(tokens_all))
            blended = blend_keep * inner + (1.0 - blend_keep) * ng_ref[own, :]
            nl_ref[own, cols] = jnp.where(picked[own] == k, blended, inner)
        stores[3 + f].start()

    for s in range(half):
        for sign, f, hops, to, d in flows:
            if s + 1 <= hops:
                w_copy(wrap(y - turn * sign * s), f, to, d).wait_send()
    for s in range(1, n_y):
        for f in range(n_parts):
            rs_copy(wrap(y + s), f, 1).wait_send()
    for i in range(3):
        t_copy(a, i, mate).wait_send()
    for k, to in plane:
        n_copy(k, to).wait_send()
        d_copy(k, to).wait_send()
    @pl.when(a != 3)
    def _():
        e_copy(a).wait_send()

    @pl.when(is_summer)
    def _():
        p_copy().wait_send()
        for t in range(1, n_z):
            z_copy(t).wait_send()
            f_copy(t).wait_send()
        for k, to in others:
            b_copy(k, to).wait_send()

    for st in stores:
        st.wait()


def finish(nl_in, ig_in, nm_in, ng_in, nl_out, ig_out, nm_out, ng_out, nl_ref, ig_ref, nm_ref, ng_ref, in_sem, out_sem):
    loads, stores = [], []
    for src, held, dst, n in (
        (ig_in, ig_ref, ig_out, 4), (nl_in, nl_ref, nl_out, 3), (nm_in, nm_ref, nm_out, 1), (ng_in, ng_ref, ng_out, 1)
    ):
        n = min(n, src.shape[0] // 16)
        size = src.shape[0] // n // 16 * 16
        for i in range(n):
            part = pl.ds(i * size, size if i < n - 1 else src.shape[0] - i * size)
            at = len(loads)
            loads.append(pltpu.make_async_copy(src.at[part, :], held.at[part, :], in_sem.at[at]))
            stores.append(pltpu.make_async_copy(held.at[part, :], dst.at[part, :], out_sem.at[at]))
    for ld in loads:
        ld.start()
    for ld, st in zip(loads, stores):
        ld.wait()
        st.start()
    for st in stores:
        st.wait()


def solution(mesh):
    n_rep, n_fsdp = mesh.shape["rep"], mesh.shape["fsdp"]
    n_y = n_fsdp // 4

    def shards(inputs, targets, local_weights, global_weights, momentum, fragment):
        x, t, lw = inputs[0], targets[0], local_weights[0]
        tok, width = x.shape
        rows, hidden = lw.shape
        quarter = width // 4
        small = global_weights.shape
        n_z = n_rep // 2
        limit = 63 * 1024 * 1024
        n_parts = min(2, rows // 16)
        smem = pl.BlockSpec(memory_space=pltpu.SMEM)
        hbm = pl.BlockSpec(memory_space=pltpu.HBM)
        dma = pltpu.SemaphoreType.DMA
        V = pltpu.VMEM
        shape = jax.ShapeDtypeStruct
        outs = pl.pallas_call(
            functools.partial(kernel, n_rep, n_y, tok * n_fsdp, n_parts),
            out_shape=(shape((rows, hidden), f32), shape((tok, width), bf16), shape(small, f32), shape(small, f32)),
            in_specs=[smem] + [hbm] * 5,
            out_specs=(hbm,) * 4,
            scratch_shapes=[
                V((rows, hidden), f32),
                V((tok, width), bf16),
                V(small, f32),
                V(small, f32),
                V((tok, width), bf16),
                V((rows, hidden), f32),
                V(small, f32),
                V(small, f32),
                V((quarter, hidden), bf16),
                V((4, tok, hidden), bf16),
                V((width, tok), bf16),
                V((4, quarter, tok), bf16),
                V((4, quarter, tok), bf16),
                V((quarter, hidden), f32),
                V((4, quarter, tok), bf16),
                V((4, quarter, tok), bf16),
                V((quarter, hidden), bf16),
                V((quarter, hidden), bf16),
                V((quarter, hidden), bf16),
                V((width, tok), bf16),
                V(small, f32),
                V(small, f32),
                V((4 * rows, small[1]), f32),
                V((n_z, 4 * rows // n_z, small[1]), f32),
                V((2, 4 * rows // n_z, small[1]), f32),
                V((4 * rows, small[1]), f32),
                dma((4 + n_parts,)), dma((3 + n_parts,)),
                dma((2, n_y, n_parts)), dma((n_y, n_parts)),
                dma((3,)), dma((4,)),
                dma((4,)), dma((4,)),
                dma((4,)), dma((4,)),
                dma((n_y, n_parts)), dma((n_y, n_parts)), dma((n_y, n_parts)),
                pltpu.SemaphoreType.REGULAR,
                dma(()), dma((4,)), dma((4,)), dma(()),
                dma((n_z,)), dma((n_z,)), dma(()), dma(()), dma((n_z,)), dma((n_z,)),
            ],
            compiler_params=pltpu.CompilerParams(
                collective_id=0, has_side_effects=True, vmem_limit_bytes=limit
            ),
        )(fragment, x, t, lw, global_weights, momentum)
        new_local, input_grad, new_m, new_g = pl.pallas_call(
            finish,
            out_shape=(shape((rows, hidden), f32), shape((tok, width), bf16), shape(small, f32), shape(small, f32)),
            in_specs=[hbm] * 4,
            out_specs=(hbm,) * 4,
            scratch_shapes=[
                V((rows, hidden), f32), V((tok, width), bf16), V(small, f32), V(small, f32), dma((9,)), dma((9,))
            ],
            compiler_params=pltpu.CompilerParams(vmem_limit_bytes=limit),
        )(*outs)
        return new_local[None], input_grad[None], new_m, new_g

    placed = (
        P("rep", "fsdp", None),
        P("rep", "fsdp", None),
        P("rep", "fsdp", None),
        P("fsdp", None),
        P("fsdp", None),
        P(),
    )
    return jax.shard_map(
        shards,
        mesh=mesh,
        in_specs=placed,
        out_specs=(
            P("rep", "fsdp", None),
            P("rep", "fsdp", None),
            P("fsdp", None),
            P("fsdp", None),
        ),
        check_vma=False,
    )
```
